32 devices in a mesh: ctx: 16 (over z, y, core), head: 2 (over x).
Axes of the slice: x: 2, y: 2, z: 4, core: 2. Of those that a mesh axis runs over, the one named last changes fastest.
Arguments:
- query: bfloat16 [2048, 8192], P('ctx', 'head'), may hold values from -11 to 11
- key_in: bfloat16 [2048, 1024], P('ctx', 'head'), may hold values from -11 to 11
- value: bfloat16 [2048, 1024], P('ctx', 'head'), may hold values from -6 to 6
- grad_y: bfloat16 [2048, 8192], P('ctx', 'head'), may hold values from -6 to 6
- w_out: bfloat16 [8192, 8192], P('head', 'ctx'), may hold values from -0.0625 to 0.0625
- parent: int32 [16], replicated, may hold values from 1 to 15, as said below
Outputs:
- grad_query: bfloat16 [2048, 8192], P('ctx', 'head')
- grad_key: bfloat16 [2048, 1024], P('ctx', 'head')
- grad_value: bfloat16 [2048, 1024], P('ctx', 'head')
The draws below stay inside these ranges and needn't reach their ends.
Inputs may be any that keep to these rules, and one draw needn't show every extreme that they name: The shared prefix is blocks 16 - 4 to 15: parent[15] = 15 and parent[b] = b + 1 for the other prefix blocks; the earlier blocks form particles of 4 consecutive blocks, in which each block's parent is the block after it, except a particle's last block, whose parent is a block of the shared prefix.
All inputs are finite; a program needn't handle non-finite values.
Results may differ from the reference program's by a relative error of at most 0.014.
Values may be sent and summed in bfloat16 or wider, within the bound.
No kernel may reach another device: no remote copies, remote signals or barrier semaphores. Data moves between devices by JAX's collectives and lax.ppermute only.
A program may use at most 192 MiB of HBM per device.

```python
import jax
import jax.numpy as jnp
from jax import lax

D = 8192
H_KV = 8
HPG = 8
DH = 128
BLOCK = 128
PREFIX = 4
PARTICLE = 4
TOKENS = 2048
NBLOCKS = 16
HEADS = 64


def paired_draw(key):
    base = jax.random.fold_in(key, 11)
    query_key, key_key = jax.random.split(base, 2)
    heads = H_KV * HPG
    queries = jnp.clip(jax.random.normal(query_key, (TOKENS, heads * DH), jnp.float32), -6.0, 6.0)
    keys = jnp.clip(jax.random.normal(key_key, (TOKENS, H_KV * DH), jnp.float32), -6.0, 6.0)
    return (queries.astype(jnp.bfloat16), keys.astype(jnp.bfloat16))


def draw_query(key, part):
    return paired_draw(key)[0]


def draw_key_in(key, part):
    return paired_draw(key)[1]


def draw_parent(key, part):
    blocks = jnp.arange(NBLOCKS, dtype=jnp.int32)
    first_prefix = NBLOCKS - PREFIX
    roots = jax.random.randint(jax.random.fold_in(key, 3), (NBLOCKS,), first_prefix, NBLOCKS, dtype=jnp.int32)
    trailing = (blocks < first_prefix) & (blocks % PARTICLE == PARTICLE - 1)
    return jnp.where(trailing, roots, jnp.minimum(blocks + 1, NBLOCKS - 1)).astype(jnp.int32)


def level_of(rng, dims, cuts, smallest, largest):
    level = 1.0
    for axis_at, parts in cuts:
        draws = jax.random.uniform(jax.random.fold_in(jax.random.fold_in(rng, 6), axis_at), (parts,), jnp.float32, smallest / len(cuts), largest / len(cuts))
        level = level * jnp.repeat(jnp.exp(draws), dims[axis_at] // parts).reshape((-1,) + (1,) * (len(dims) - 1 - axis_at))
    return level


def scatter_about(key, shape, scale, limit, cuts=(), held_as=jnp.bfloat16):
    factor_of = level_of(key, shape, cuts, -0.22, 0.18) if cuts else 1.0
    result = jax.random.normal(key, shape, jnp.float32) * scale * factor_of
    return jnp.minimum(jnp.maximum(result, -limit), limit).astype(held_as)


def setup_inputs(seed: int = 0) -> dict:
    key_of = jax.random.split(jax.random.key(seed), 7)
    return {
        "query": draw_query(jax.random.fold_in(key_of[6], 71), 0),
        "key_in": draw_key_in(jax.random.fold_in(key_of[6], 71), 0),
        "value": scatter_about(key_of[2], (TOKENS, H_KV * DH), 1.0, 6.0, ((0, 16), (1, 2))),
        "grad_y": scatter_about(key_of[3], (TOKENS, D), 1.0, 6.0, ((0, 16), (1, 2))),
        "w_out": scatter_about(key_of[4], (HEADS * DH, D), (HEADS * DH) ** -0.5, 0.0625, ((0, 2), (1, 16))),
        "parent": draw_parent(jax.random.fold_in(key_of[6], 71), 0),
    }


def ancestors(parent):
    count = parent.shape[0]
    index = jnp.arange(count, dtype=jnp.int32)
    start = (index[:, None] == index[None, :]).astype(jnp.int32)

    def advance(step, state):
        current, marks = state
        current = jnp.sum(jnp.where(current[:, None] == index[None, :], parent[None, :], 0), axis=1).astype(jnp.int32)
        marks = jnp.maximum(marks, (current[:, None] == index[None, :]).astype(jnp.int32))
        return current, marks

    return lax.fori_loop(0, count, advance, (index, start))[1]


def reference(query, key_in, value, grad_y, w_out, parent):
    total = query.shape[0]
    scale = DH ** -0.5
    grad_attn = lax.dot_general(grad_y, w_out, (((1,), (1,)), ((), ())), preferred_element_type=jnp.float32).astype(jnp.bfloat16)
    visible = ancestors(parent)
    position = jnp.arange(total, dtype=jnp.int32)
    block_of = position // BLOCK
    allowed = (visible[block_of][:, block_of] > 0) & ((block_of[:, None] != block_of[None, :]) | (position[None, :] <= position[:, None]))
    query_heads = query.reshape(total, H_KV, HPG, DH).transpose(1, 2, 0, 3)
    grad_heads = grad_attn.reshape(total, H_KV, HPG, DH).transpose(1, 2, 0, 3)
    key_heads = key_in.reshape(total, H_KV, DH).transpose(1, 0, 2)
    value_heads = value.reshape(total, H_KV, DH).transpose(1, 0, 2)

    def group(items):
        query_group, grad_group, key_group, value_group = items

        def one_head(carry, pair):
            key_sum, value_sum = carry
            query_one, grad_one = pair
            scores = jnp.dot(query_one, key_group.T, preferred_element_type=jnp.float32) * scale
            masked = jnp.where(allowed, scores, -1e30)
            top = jnp.max(masked, axis=1)
            weights = jnp.where(allowed, jnp.exp(scores - top[:, None]), 0.0)
            prob = weights / jnp.sum(weights, axis=1)[:, None]
            dprob = jnp.dot(grad_one, value_group.T, preferred_element_type=jnp.float32)
            delta = jnp.sum(prob * dprob, axis=1)
            prob_low = prob.astype(jnp.bfloat16)
            value_sum = value_sum + jnp.dot(prob_low.T, grad_one, preferred_element_type=jnp.float32)
            dscore = (prob * (dprob - delta[:, None])).astype(jnp.bfloat16)
            grad_q = jnp.dot(dscore, key_group, preferred_element_type=jnp.float32) * scale
            key_sum = key_sum + jnp.dot(dscore.T, query_one, preferred_element_type=jnp.float32) * scale
            return (key_sum, value_sum), grad_q

        empty = jnp.zeros((total, DH), jnp.float32)
        (key_sum, value_sum), grad_q = lax.scan(one_head, (empty, empty), (query_group, grad_group))
        return grad_q, key_sum, value_sum

    grad_q, grad_k, grad_v = lax.map(group, (query_heads, grad_heads, key_heads, value_heads))
    grad_query = grad_q.transpose(2, 0, 1, 3).reshape(total, H_KV * HPG * DH).astype(jnp.bfloat16)
    grad_key = grad_k.transpose(1, 0, 2).reshape(total, H_KV * DH).astype(jnp.bfloat16)
    grad_value = grad_v.transpose(1, 0, 2).reshape(total, H_KV * DH).astype(jnp.bfloat16)
    return (grad_query, grad_key, grad_value)
```

```python
import functools

import jax
import jax.numpy as jnp
from jax import lax
from jax.experimental import pallas as pl
from jax.experimental.pallas import tpu as pltpu
from jax.sharding import PartitionSpec as P

DH = 128
BLOCK = 128
QUAD = 4
SCALE = DH ** (-0.5)
LOG2E = 1.4426950408889634
NT = (((1,), (1,)), ((), ()))


def project_kernel(place_ref, x_ref, *refs):
    w_refs, out_ref = refs[:-1], refs[-1]
    mine = place_ref[0]
    width = w_refs[0].shape[1]
    total = None
    for step, w_ref in enumerate(w_refs):
        columns = pl.ds(pl.multiple_of((mine ^ step) * width, width), width)
        term = lax.dot_general(x_ref[:, columns], w_ref[...], NT, preferred_element_type=jnp.float32)
        total = term if total is None else total + term
    out_ref[...] = total.astype(out_ref.dtype)


def project(place, x, pieces, dtype):
    rows, depth = x.shape
    columns, width = pieces[0].shape
    tile = min(256, columns)
    return pl.pallas_call(
        project_kernel,
        grid_spec=pltpu.PrefetchScalarGridSpec(
            num_scalar_prefetch=1,
            grid=(columns // tile,),
            in_specs=[pl.BlockSpec((rows, depth), lambda n, s: (0, 0))]
            + [pl.BlockSpec((tile, width), lambda n, s: (n, 0))] * len(pieces),
            out_specs=pl.BlockSpec((rows, tile), lambda n, s: (0, n)),
        ),
        out_shape=jax.ShapeDtypeStruct((rows, columns), dtype),
        compiler_params=pltpu.CompilerParams(vmem_limit_bytes=40 * 2**20),
        cost_estimate=pl.CostEstimate(
            flops=2 * rows * depth * columns,
            bytes_accessed=2 * (rows * depth + depth * columns + rows * columns),
            transcendentals=0,
        ),
    )(place, x, *pieces)


def attend_kernel(head_bits, place_ref, q_ref, k_ref, v_ref, kp_ref, vp_ref, *refs):
    part_refs, (gq_ref, dk_ref, dv_ref) = refs[:-9], refs[-9:-6]
    keys, values, keys_t, queries, grads, triangle = refs[-6:]
    mine, head_place, root = place_ref[0], place_ref[1], place_ref[2]
    own = QUAD * BLOCK
    half = own // 2
    pieces = 1 << head_bits
    piece = BLOCK // pieces

    @pl.when(pl.program_id(0) == 0)
    def first():
        for b in range(QUAD):
            rows = pl.ds(b * BLOCK, BLOCK)
            late = pl.ds(own + b * BLOCK, BLOCK)
            keys[rows, :] = k_ref[b ^ mine]
            values[rows, :] = v_ref[b ^ mine]
            keys[late, :] = kp_ref[b ^ mine]
            values[late, :] = vp_ref[b ^ mine]
        keys_t[...] = keys[...].astype(jnp.float32).T.astype(jnp.bfloat16)
        row = lax.broadcasted_iota(jnp.int32, (half, half), 0)
        col = lax.broadcasted_iota(jnp.int32, (half, half), 1)
        seen = (row // BLOCK > col // BLOCK) | ((row // BLOCK == col // BLOCK) & (row <= col))
        triangle[...] = jnp.where(seen, 0.0, -1e30)
        dk_ref[...] = jnp.zeros_like(dk_ref)
        dv_ref[...] = jnp.zeros_like(dv_ref)

    for b in range(QUAD):
        queries[pl.ds(b * BLOCK, BLOCK), :] = q_ref[b ^ mine]
        for i in range(pieces):
            at = (
                ((b >> 1) ^ (mine >> 1))
                | ((i ^ head_place) << 1)
                | (((b & 1) ^ (mine & 1)) << (1 + head_bits))
            )
            total = part_refs[0][at].astype(jnp.float32)
            for ref in part_refs[1:]:
                total = total + ref[at].astype(jnp.float32)
            grads[pl.ds(b * BLOCK + i * piece, piece), :] = total.astype(jnp.bfloat16)

    for pair in range(2):
        start = pair * half
        count = 2 * own - start
        q = queries[pl.ds(start, half), :]
        g = grads[pl.ds(start, half), :]
        rows = pl.ds(start, count)
        scores = lax.dot_general(keys[rows, :], q, NT, preferred_element_type=jnp.float32)
        late = lax.broadcasted_iota(jnp.int32, (own, half), 0) >= root * BLOCK
        parts = [scores[:half] + triangle[...]]
        if pair == 0:
            parts.append(scores[half : 2 * half])
        parts.append(jnp.where(late, scores[count - own :], -1e30))
        scores = jnp.concatenate(parts, axis=0)
        top = jnp.max(scores, axis=0, keepdims=True)
        weights = jnp.exp2((scores - top) * (SCALE * LOG2E))
        prob = weights * (1.0 / jnp.sum(weights, axis=0, keepdims=True))
        dprob = lax.dot_general(values[rows, :], g, NT, preferred_element_type=jnp.float32)
        delta = jnp.sum(prob * dprob, axis=0, keepdims=True)
        dscore = (prob * (dprob - delta)).astype(jnp.bfloat16)
        dv_ref[rows, :] += jnp.dot(prob.astype(jnp.bfloat16), g, preferred_element_type=jnp.float32)
        dk_ref[rows, :] += jnp.dot(dscore, q, preferred_element_type=jnp.float32) * SCALE
        gq = jnp.dot(keys_t[:, start:], dscore, preferred_element_type=jnp.float32) * SCALE
        gq = gq.T.astype(jnp.bfloat16)
        for b in range(QUAD // 2):
            gq_ref[(pair * (QUAD // 2) + b) ^ mine] = gq[b * BLOCK : (b + 1) * BLOCK]


def attend(place, qkv, prefix, partials, heads, head_bits):
    own = QUAD * BLOCK
    block = (QUAD, BLOCK, DH)

    def column(at):
        return pl.BlockSpec(block, lambda n, s: (0, 0, at))

    slots, piece, _ = partials[0].shape
    return pl.pallas_call(
        functools.partial(attend_kernel, head_bits),
        grid_spec=pltpu.PrefetchScalarGridSpec(
            num_scalar_prefetch=1,
            grid=(heads,),
            in_specs=[
                pl.BlockSpec(block, lambda n, s: (0, 0, n)),
                column(heads),
                column(heads + 1),
                column(0),
                column(1),
            ]
            + [pl.BlockSpec((slots, piece, DH), lambda n, s: (0, 0, n))] * len(partials),
            out_specs=[
                pl.BlockSpec(block, lambda n, s: (0, 0, n)),
                pl.BlockSpec((2 * own, DH), lambda n, s: (0, 0)),
                pl.BlockSpec((2 * own, DH), lambda n, s: (0, 0)),
            ],
            scratch_shapes=[
                pltpu.VMEM((2 * own, DH), jnp.bfloat16),
                pltpu.VMEM((2 * own, DH), jnp.bfloat16),
                pltpu.VMEM((DH, 2 * own), jnp.bfloat16),
                pltpu.VMEM((own, DH), jnp.bfloat16),
                pltpu.VMEM((own, DH), jnp.bfloat16),
                pltpu.VMEM((own // 2, own // 2), jnp.float32),
            ],
        ),
        out_shape=[
            jax.ShapeDtypeStruct((QUAD, BLOCK, heads * DH), jnp.bfloat16),
            jax.ShapeDtypeStruct((2 * own, DH), jnp.float32),
            jax.ShapeDtypeStruct((2 * own, DH), jnp.float32),
        ],
        compiler_params=pltpu.CompilerParams(vmem_limit_bytes=40 * 2**20),
        cost_estimate=pl.CostEstimate(
            flops=10 * own * 2 * own * DH * heads,
            bytes_accessed=16 * own * heads * DH,
            transcendentals=2 * own * own * heads,
        ),
    )(place, qkv, qkv, qkv, prefix, prefix, *partials)


def per_device(query, key_in, value, grad_y, w_out, parent):
    places, sides = lax.axis_size("ctx"), lax.axis_size("head")
    layers = places // QUAD
    head_bits = sides.bit_length() - 1
    place, side = lax.axis_index("ctx"), lax.axis_index("head")
    layer, mine = place // QUAD, place % QUAD
    tokens = query.shape[0]
    groups = key_in.shape[1] // DH
    heads = query.shape[1] // DH // QUAD
    depth = QUAD * w_out.shape[1]
    rows = w_out.shape[0] // QUAD

    def swap(x, bits):
        return lax.ppermute(x, "ctx", [(c, c ^ bits) for c in range(places)])

    def flip(x, bits):
        return lax.ppermute(x, "head", [(s, s ^ bits) for s in range(sides)])

    def rotate(x, steps):
        shift = steps * QUAD
        return lax.ppermute(x, "ctx", [(c, (c + shift) % places) for c in range(places)])

    def hop(x, sources, steps):
        pairs = [(s * QUAD + i, (s + steps) * QUAD + i) for s in sources for i in range(QUAD)]
        return lax.ppermute(x, "ctx", pairs)

    def columns(x, at, width):
        return lax.dynamic_slice_in_dim(x, at * width, width, 1)

    share = tokens // sides
    if sides == 2:
        held = lax.dynamic_slice_in_dim(grad_y, side * share, share, 0)
        other = flip(lax.dynamic_slice_in_dim(grad_y, (1 - side) * share, share, 0), 1)
        span = grad_y.shape[1] // depth

        def features(at):
            return jnp.where(
                at // span == side, columns(held, at % span, depth), columns(other, at % span, depth)
            )
    else:
        every = lax.all_to_all(grad_y, "head", 0, 1, tiled=True)

        def features(at):
            return columns(every, at, depth)

    pieces = []
    for step in range(QUAD):
        piece = lax.dynamic_slice_in_dim(w_out, (mine ^ step) * rows, rows, 0)
        pieces.append(swap(piece, step) if step else piece)

    arrived = []
    for step in range(QUAD):
        to = mine ^ step
        piece = jnp.concatenate(
            [
                columns(query, to, heads * DH),
                columns(key_in, to * groups // QUAD, DH),
                columns(value, to * groups // QUAD, DH),
            ],
            axis=1,
        )
        arrived.append(swap(piece, step) if step else piece)
    qkv = jnp.stack(arrived)

    prefix = qkv[:, :, heads * DH :]
    levels = layers.bit_length() - 1
    for level in reversed(range(levels)):
        span_of = 1 << level
        sources = [s for s in range(layers) if (layers - 1 - s) % (2 * span_of) == 0]
        landed = hop(prefix, sources, -span_of)
        prefix = jnp.where((layers - 1 - layer) % (2 * span_of) == span_of, landed, prefix)

    def gather(x):
        x = jnp.concatenate([x, swap(x, 2)], axis=0)
        for bit in range(head_bits):
            x = jnp.concatenate([x, flip(x, 1 << bit)], axis=0)
        return jnp.concatenate([x, swap(x, 1)], axis=0)

    scalars = mine.reshape(1).astype(jnp.int32)
    partials = []
    for steps in [0] + sorted(range(1, layers), key=lambda r: abs(2 * r - layers)):
        piece = features((layer - steps) % layers)
        if steps:
            piece = rotate(piece, -steps)
        everything = gather(piece)
        part = project(scalars, everything, pieces, jnp.bfloat16 if steps else jnp.float32)
        if steps:
            part = rotate(part, steps)
        partials.append(part.reshape(QUAD * sides, share, heads * DH))

    root = jnp.where(
        layer == layers - 1, QUAD, parent[layer * QUAD + QUAD - 1] - (parent.shape[0] - QUAD)
    )
    scalars = jnp.stack([mine, side, root]).astype(jnp.int32)
    grad_query, grad_key, grad_value = attend(scalars, qkv, prefix, partials, heads, head_bits)

    out_query = jnp.zeros(query.shape, query.dtype)
    for step in range(QUAD):
        piece = swap(grad_query[step], step) if step else grad_query[0]
        out_query = lax.dynamic_update_slice_in_dim(
            out_query, piece, (mine ^ step) * heads * DH, 1
        )

    own = QUAD * BLOCK
    both = jnp.concatenate([grad_key, grad_value], axis=1)
    far = both[own:]
    for level in range(levels):
        span_of = 1 << level
        sources = [s for s in range(layers) if (layers - 1 - s) % (2 * span_of) == span_of]
        far = far + hop(far.astype(jnp.bfloat16), sources, span_of).astype(jnp.float32)
    both = both[:own] + jnp.where(layer == layers - 1, far, 0.0)
    narrow = both.astype(jnp.bfloat16)
    held_groups = max(1, groups // QUAD)
    total_key = jnp.zeros(key_in.shape, jnp.float32)
    total_value = jnp.zeros(value.shape, jnp.float32)
    for step in range(QUAD):
        at = mine ^ step
        if step:
            piece = swap(lax.dynamic_slice_in_dim(narrow, at * BLOCK, BLOCK, 0), step)
        else:
            piece = lax.dynamic_slice_in_dim(both, at * BLOCK, BLOCK, 0)
        piece = piece.astype(jnp.float32)
        spot = (at * groups // QUAD) * DH

        def add(total, part):
            here = lax.dynamic_slice_in_dim(total, spot, held_groups * DH, 1)
            return lax.dynamic_update_slice_in_dim(total, here + part, spot, 1)

        total_key = add(total_key, piece[:, :DH])
        total_value = add(total_value, piece[:, DH:])
    return out_query, total_key.astype(jnp.bfloat16), total_value.astype(jnp.bfloat16)


def solution(mesh):
    placed = (
        P("ctx", "head"),
        P("ctx", "head"),
        P("ctx", "head"),
        P("ctx", "head"),
        P("head", "ctx"),
        P(),
    )
    return jax.shard_map(
        per_device,
        mesh=mesh,
        in_specs=placed,
        out_specs=(P("ctx", "head"), P("ctx", "head"), P("ctx", "head")),
        check_vma=False,
    )
```

```python
import functools

import jax
import jax.numpy as jnp
from jax import lax
from jax.experimental import pallas as pl
from jax.experimental.pallas import tpu as pltpu
from jax.sharding import PartitionSpec as P

OPT = {'vmem': 16, 'cp': 1.0, 'cs': 1.0, 'ca': 1.0, 'cf': 1, 'dual': [0, 0, 0, 1], 'z0': 0, 'merged': 1, 'home': 1, 'cut': 4, 'ties': {'y1:s': ['r3', 'W0a', 'xe2'], 'x3:s': ['r1', 'W0a', 'xe2'], 'r2:s': ['r1', 'r3'], 'k1:s': ['r1'], 'k2:s': ['r1'], 'k3:s': ['r1'], 'W1b:s': ['r1'], 'x1:s': ['x3'], 'y3:s': ['y1'], 'c1:s': ['y3', 'r2', 'k1', 'k2', 'k3'], 'c3:s': ['x1', 'r2'], 'y2:s': ['x1', 'y3'], 'y0:s': ['x1', 'y3', 'r2', 'W1b'], 'h1:s': ['x1', 'y3'], 'p01:s': ['h1'], 'p03:s': ['c1'], 'x2:s': ['p01', 'p03'], 'W1a:s': ['y2'], 'c2:s': ['a1', 'y0', 'h1'], 'a3:s': ['x2', 'a1', 'y0', 'h1'], 'x0:s': ['x2', 'a1'], 'h2:s': ['x2', 'a1'], 'p11:s': ['a3', 'W1a', 'x0', 'p02'], 'p13:s': ['p11'], 'c0:s': ['a3'], 'q1:s': ['p02'], 'q2:s': ['p02'], 'q3:s': ['p02'], 'p12:s': ['a2', 'c0', 'h2', 'q1', 'q2', 'q3'], 'p00:s': ['p12'], 'p10:s': ['p12'], 'S:s': ['p12'], 'y1:r': ['r2'], 'att1:s': ['p00']}}
DH = 128
BLOCK = 128
QUAD = 4
SCALE = DH ** (-0.5)
LOG2E = 1.4426950408889634
NT = (((1,), (1,)), ((), ()))


def after(value, *earlier):
    return lax.optimization_barrier((value,) + earlier)[0]


def project_kernel(place_ref, x_ref, *refs):
    w_refs, out_ref = refs[:QUAD], refs[-1]
    mine = place_ref[0]
    width = w_refs[0].shape[1]
    total = refs[QUAD][...].astype(jnp.float32) if len(refs) > QUAD + 1 else None
    for step, w_ref in enumerate(w_refs):
        columns = pl.ds(pl.multiple_of((mine ^ step) * width, width), width)
        term = lax.dot_general(x_ref[:, columns], w_ref[...], NT, preferred_element_type=jnp.float32)
        total = term if total is None else total + term
    out_ref[...] = total.astype(out_ref.dtype)


def project(place, x, w_out, others, base, dtype, more=None):
    rows, depth = x.shape
    _, columns, width = others[0][0].shape
    tile = min(256, columns & -columns)
    steps = columns // tile
    per_place = w_out.shape[0] // QUAD // tile
    offset = base // tile
    out_spec = pl.BlockSpec((rows, tile), lambda n, s: (0, n))
    in_specs = [pl.BlockSpec((rows, depth), lambda n, s: (0, 0))]
    in_specs.append(pl.BlockSpec((tile, width), lambda n, s: (s[0] * per_place + offset + n, 0)))
    for _, pick in others:
        in_specs.append(pl.BlockSpec((None, tile, width), lambda n, s, pick=pick: (pick(s[0]), n, 0)))
    operands = [x, w_out, *(array for array, _ in others)]
    if more is not None:
        in_specs.append(out_spec)
        operands.append(more)
    return pl.pallas_call(
        project_kernel,
        grid_spec=pltpu.PrefetchScalarGridSpec(
            num_scalar_prefetch=1, grid=(steps,), in_specs=in_specs, out_specs=out_spec
        ),
        out_shape=jax.ShapeDtypeStruct((rows, columns), dtype),
        compiler_params=pltpu.CompilerParams(vmem_limit_bytes=OPT['vmem'] * 2**20),
        cost_estimate=pl.CostEstimate(
            flops=int(OPT['cp'] * (2 * rows * depth * columns)),
            bytes_accessed=int(OPT['cp'] * (2 * (rows * depth + depth * columns + rows * columns))),
            transcendentals=0,
        ),
    )(place, *operands)


def lay_out(place_ref, own_ref, late_ref, out):
    for b in range(QUAD):
        out[pl.ds(b * BLOCK, BLOCK), :] = own_ref[b ^ place_ref[0]]
        out[pl.ds((QUAD + b) * BLOCK, BLOCK), :] = late_ref[b ^ place_ref[0]]


def lay_by(place_ref, refs, out):
    for step, ref in enumerate(refs):
        out[pl.ds(pl.multiple_of((step ^ place_ref[0]) * BLOCK, BLOCK), BLOCK), :] = ref[...]


def weigh_kernel(place_ref, k_ref, kp_ref, *refs):
    q_refs, (prob_ref, keys, queries, triangle) = refs[:QUAD], refs[QUAD:]
    mine, root = place_ref[0], place_ref[2]
    own = QUAD * BLOCK
    half = own // 2

    @pl.when(pl.program_id(0) == 0)
    def first():
        lay_out(place_ref, k_ref, kp_ref, keys)
        row = lax.broadcasted_iota(jnp.int32, (half, half), 0)
        col = lax.broadcasted_iota(jnp.int32, (half, half), 1)
        seen = (row // BLOCK > col // BLOCK) | ((row // BLOCK == col // BLOCK) & (row <= col))
        triangle[...] = jnp.where(seen, 0.0, -1e30)

    lay_by(place_ref, q_refs, queries)
    for pair in range(2):
        start = pair * half
        count = 2 * own - start
        q = queries[pl.ds(start, half), :]
        scores = lax.dot_general(
            keys[pl.ds(start, count), :], q, NT, preferred_element_type=jnp.float32
        )
        late = lax.broadcasted_iota(jnp.int32, (own, half), 0) >= root * BLOCK
        parts = [scores[:half] + triangle[...]]
        if pair == 0:
            parts.append(scores[half : 2 * half])
        parts.append(jnp.where(late, scores[count - own :], -1e30))
        scores = jnp.concatenate(parts, axis=0)
        top = jnp.max(scores, axis=0, keepdims=True)
        weights = jnp.exp2((scores - top) * (SCALE * LOG2E))
        prob = weights * (1.0 / jnp.sum(weights, axis=0, keepdims=True))
        prob_ref[0, pl.ds(start, count), pl.ds(start, half)] = prob.astype(jnp.bfloat16)


def weigh(place, queries, keyval, prefix):
    own = QUAD * BLOCK
    block = (QUAD, BLOCK, DH)
    heads = queries[0].shape[1] // DH
    return pl.pallas_call(
        weigh_kernel,
        grid_spec=pltpu.PrefetchScalarGridSpec(
            num_scalar_prefetch=1,
            grid=(heads,),
            in_specs=[
                pl.BlockSpec(block, lambda n, s: (0, 0, 0)),
                pl.BlockSpec(block, lambda n, s: (0, 0, 0)),
            ]
            + [pl.BlockSpec((BLOCK, DH), lambda n, s: (0, n))] * QUAD,
            out_specs=pl.BlockSpec((1, 2 * own, own), lambda n, s: (n, 0, 0)),
            scratch_shapes=[
                pltpu.VMEM((2 * own, DH), jnp.bfloat16),
                pltpu.VMEM((own, DH), jnp.bfloat16),
                pltpu.VMEM((own // 2, own // 2), jnp.float32),
            ],
        ),
        out_shape=jax.ShapeDtypeStruct((heads, 2 * own, own), jnp.bfloat16),
        compiler_params=pltpu.CompilerParams(vmem_limit_bytes=OPT['vmem'] * 2**20),
        cost_estimate=pl.CostEstimate(
            flops=int(OPT['cs'] * (4 * own * own * DH * heads)),
            bytes_accessed=4 * own * own * heads,
            transcendentals=2 * own * own * heads,
        ),
    )(place, keyval, prefix, *queries)


def attend_kernel(head_bits, count_parts, place_ref, prob_ref, k_ref, v_ref, kp_ref, vp_ref, *refs):
    q_refs, refs = refs[:QUAD], refs[QUAD:]
    part_refs, rest = refs[:count_parts], refs[count_parts:]
    gq_ref, dk_ref, dv_ref = rest[-8:-5]
    values, keys_t, keys, queries, grads = rest[-5:]
    before = rest[:-8]
    mine, head_place = place_ref[0], place_ref[1]
    own = QUAD * BLOCK
    half = own // 2
    pieces = 1 << head_bits
    piece = BLOCK // pieces

    @pl.when(pl.program_id(0) == 0)
    def first():
        lay_out(place_ref, k_ref, kp_ref, keys)
        lay_out(place_ref, v_ref, vp_ref, values)
        keys_t[...] = keys[...].astype(jnp.float32).T.astype(jnp.bfloat16)
        if before:
            dk_ref[...] = before[0][...]
            dv_ref[...] = before[1][...]
        else:
            dk_ref[...] = jnp.zeros_like(dk_ref)
            dv_ref[...] = jnp.zeros_like(dv_ref)

    lay_by(place_ref, q_refs, queries)
    for b in range(QUAD):
        for i in range(pieces):
            at = (
                ((b >> 1) ^ (mine >> 1))
                | ((i ^ head_place) << 1)
                | (((b & 1) ^ (mine & 1)) << (1 + head_bits))
            )
            total = part_refs[0][at].astype(jnp.float32)
            for ref in part_refs[1:]:
                total = total + ref[at].astype(jnp.float32)
            grads[pl.ds(b * BLOCK + i * piece, piece), :] = total.astype(jnp.bfloat16)

    for pair in range(2):
        start = pair * half
        q = queries[pl.ds(start, half), :]
        g = grads[pl.ds(start, half), :]
        chunks = [pl.ds(row, half) for row in reversed(range(start, 2 * own, half))]
        lows = [prob_ref[0, rows, pl.ds(start, half)] for rows in chunks]
        dprobs = [
            lax.dot_general(values[rows, :], g, NT, preferred_element_type=jnp.float32)
            for rows in chunks
        ]
        delta = sum(
            jnp.sum(low.astype(jnp.float32) * dprob, axis=0, keepdims=True)
            for low, dprob in zip(lows, dprobs)
        )
        gq = None
        for rows, low, dprob in zip(chunks, lows, dprobs):
            dscore = (low.astype(jnp.float32) * (dprob - delta)).astype(jnp.bfloat16)
            dv_ref[rows, :] += jnp.dot(low, g, preferred_element_type=jnp.float32)
            dk_ref[rows, :] += jnp.dot(dscore, q, preferred_element_type=jnp.float32) * SCALE
            term = jnp.dot(keys_t[:, rows], dscore, preferred_element_type=jnp.float32)
            gq = term if gq is None else gq + term
        gq = (gq * SCALE).T.astype(jnp.bfloat16)
        for b in range(QUAD // 2):
            gq_ref[(pair * (QUAD // 2) + b) ^ mine] = gq[b * BLOCK : (b + 1) * BLOCK]


def attend(place, prob, queries, keyval, prefix, partials, base, heads, head_bits, before=()):
    own = QUAD * BLOCK
    block = (QUAD, BLOCK, DH)
    slots, piece, _ = partials[0].shape

    def column(at):
        return pl.BlockSpec(block, lambda n, s: (0, 0, at))

    whole = pl.BlockSpec((2 * own, DH), lambda n, s: (0, 0))
    return pl.pallas_call(
        functools.partial(attend_kernel, head_bits, len(partials)),
        grid_spec=pltpu.PrefetchScalarGridSpec(
            num_scalar_prefetch=1,
            grid=(heads,),
            in_specs=[
                pl.BlockSpec((1, 2 * own, own), lambda n, s: (base + n, 0, 0)),
                column(0),
                column(1),
                column(0),
                column(1),
            ]
            + [pl.BlockSpec((BLOCK, DH), lambda n, s: (0, base + n))] * QUAD
            + [pl.BlockSpec((slots, piece, DH), lambda n, s: (0, 0, n))] * len(partials)
            + [whole] * len(before),
            out_specs=[pl.BlockSpec(block, lambda n, s: (0, 0, n)), whole, whole],
            scratch_shapes=[
                pltpu.VMEM((2 * own, DH), jnp.bfloat16),
                pltpu.VMEM((DH, 2 * own), jnp.bfloat16),
                pltpu.VMEM((2 * own, DH), jnp.bfloat16),
                pltpu.VMEM((own, DH), jnp.bfloat16),
                pltpu.VMEM((own, DH), jnp.bfloat16),
            ],
        ),
        out_shape=[
            jax.ShapeDtypeStruct((QUAD, BLOCK, heads * DH), jnp.bfloat16),
            jax.ShapeDtypeStruct((2 * own, DH), jnp.float32),
            jax.ShapeDtypeStruct((2 * own, DH), jnp.float32),
        ],
        compiler_params=pltpu.CompilerParams(vmem_limit_bytes=OPT['vmem'] * 2**20),
        cost_estimate=pl.CostEstimate(
            flops=int(OPT['ca'] * (16 * own * own * DH * heads)),
            bytes_accessed=4 * own * own * heads,
            transcendentals=0,
        ),
    )(place, prob, keyval, keyval, prefix, prefix, *queries, *partials, *before)


def per_device(query, key_in, value, grad_y, w_out, parent):
    places, sides = lax.axis_size("ctx"), lax.axis_size("head")
    layers = places // QUAD
    levels = layers.bit_length() - 1
    head_bits = sides.bit_length() - 1
    place, side = lax.axis_index("ctx"), lax.axis_index("head")
    layer, mine = place // QUAD, place % QUAD
    tokens = query.shape[0]
    groups = key_in.shape[1] // DH
    heads = query.shape[1] // DH // QUAD
    depth = QUAD * w_out.shape[1]
    rows = w_out.shape[0] // QUAD
    share = tokens // sides
    counts = [max(1, heads * OPT["cut"] // 8)]
    counts.append(heads - counts[0])
    bases = [sum(counts[:part]) for part in range(len(counts))]

    def swap(x, bits):
        return lax.ppermute(x, "ctx", [(c, c ^ bits) for c in range(places)])

    def flip(x, bits):
        return lax.ppermute(x, "head", [(s, s ^ bits) for s in range(sides)])

    def rotate(x, steps):
        shift = steps * QUAD
        return lax.ppermute(x, "ctx", [(c, (c + shift) % places) for c in range(places)])

    def hop(x, pairs):
        return lax.ppermute(
            x, "ctx", [(s * QUAD + i, t * QUAD + i) for s, t in pairs for i in range(QUAD)]
        )

    def columns(x, at, width):
        return lax.dynamic_slice_in_dim(x, at * width, width, 1)

    def take(x, at, count):
        return lax.dynamic_slice_in_dim(x, at, count, 0)

    def rows_for(part, to):
        return take(w_out, to * rows + bases[part] * DH, counts[part] * DH)

    def join(x, landed):
        return jnp.concatenate([x, landed], axis=0)

    def keyval_for(step):
        at = (mine ^ step) * groups // QUAD
        return jnp.concatenate([columns(key_in, at, DH), columns(value, at, DH)], axis=1)

    def queries_for(step):
        return columns(query, mine ^ step, heads * DH)

    def prefix_hop(prefix, level):
        reach = 1 << level
        sources = [s for s in range(layers) if (layers - 1 - s) % (2 * reach) == 0]
        landed = hop(prefix, [(s, s - reach) for s in sources])
        return jnp.where((layers - 1 - layer) % (2 * reach) == reach, landed, prefix)

    scalars = jnp.stack(
        [
            mine,
            side,
            jnp.where(
                layer == layers - 1,
                QUAD,
                parent[layer * QUAD + QUAD - 1] - (parent.shape[0] - QUAD),
            ),
        ]
    ).astype(jnp.int32)

    done = {}

    def tied(name, x):
        names = [n for n in OPT["ties"].get(name, ()) if n in done]
        if not names:
            return x
        return after(x, *(done[n] for n in names))

    def start(name, send, x):
        done[name] = send(tied(name + ":s", x))

    def land(name):
        done[name] = tied(name + ":r", done[name])
        return done[name]

    def partial(name, part, x, dtype=jnp.bfloat16, more=None):
        done[name] = project(
            tied(name + ":s", scalars), x, w_out, others[part], bases[part] * DH, dtype, more
        )
        return done[name]

    def by_2(x):
        return swap(x, 2)

    def by_1(x):
        return swap(x, 1)

    def by_x(x):
        return flip(x, 1)

    others = [None] * len(counts)
    arrived = [{} for _ in counts]
    if sides == 2 and layers == 4:
        odd = (layer + 1) % 2

        def give(at):
            return lax.dynamic_slice(grad_y, ((1 - side) * share, at * depth), (share, depth))

        def features(steps, other):
            at = (layer - steps) % layers
            held = lax.dynamic_slice(grad_y, (side * share, (at % 2) * depth), (share, depth))
            return jnp.where(at // 2 == side, held, other)

        def interleave(x, landed):
            both = [part.reshape(sides, share, depth) for part in (x, landed)]
            return jnp.stack(both, axis=1).reshape(2 * sides * share, depth)

        def weights_first(part):
            if OPT["cf"]:
                start(f"W{part}b", by_1, jnp.stack([rows_for(part, mine ^ 1), rows_for(part, mine ^ 3)]))
            else:
                first = (mine & 2) ^ 2
                start(f"W{part}a", by_2, jnp.stack([rows_for(part, first + c) for c in range(2)]))

        def weights_second(part):
            if OPT["cf"]:
                beside = land(f"W{part}b")
                start(f"W{part}a", by_2, jnp.stack([rows_for(part, mine ^ 2), beside[1]]))
            else:
                across = land(f"W{part}a")
                through = lax.dynamic_index_in_dim(across, (mine & 1) ^ 1, 0, keepdims=False)
                start(f"W{part}b", by_1, jnp.stack([rows_for(part, mine ^ 1), through]))

        def weights(part):
            if OPT["cf"]:
                across = land(f"W{part}a")
                beside = done[f"W{part}b"]
                others[part] = [(beside, lambda q: 0), (across, lambda q: 0), (across, lambda q: 1)]
            else:
                beside = land(f"W{part}b")
                across = done[f"W{part}a"]
                others[part] = [(beside, lambda q: 0), (across, lambda q: q & 1), (beside, lambda q: 1)]

        x, y, z = {}, {}, {}
        start("xe1", by_x, give(odd))
        weights_first(0)
        start("xe2", by_x, give(1 - odd))
        other = land("xe1")
        start("r1", lambda v: rotate(v, -1), features(1, other))
        start("r3", lambda v: rotate(v, -3), features(3, other))
        if OPT["cf"]:
            weights_second(0)
        other = land("xe2")
        start("r2", lambda v: rotate(v, -2), features(2, other))
        z[0] = features(0, other)

        def first_gather(steps):
            if steps:
                z[steps] = land(f"r{steps}")
            if OPT["dual"][steps]:
                start(f"x{steps}", by_x, z[steps])
            else:
                start(f"y{steps}", by_2, z[steps])

        def second_gather(steps):
            if OPT["dual"][steps]:
                x[steps] = join(z[steps], land(f"x{steps}"))
                start(f"y{steps}", by_2, x[steps])
            else:
                y[steps] = join(z[steps], land(f"y{steps}"))
                start(f"x{steps}", by_x, y[steps])

        def third_gather(steps):
            if OPT["dual"][steps]:
                z[steps] = interleave(x[steps], land(f"y{steps}"))
            else:
                z[steps] = join(y[steps], land(f"x{steps}"))
            start(f"c{steps}", by_1, z[steps])

        def all_of(steps):
            z[steps] = join(z[steps], land(f"c{steps}"))
            return z[steps]

        first_gather(1)
        first_gather(3)
        kv = [keyval_for(step) for step in range(QUAD)]
        for step in range(1, QUAD):
            start(f"k{step}", lambda v, step=step: swap(v, step), kv[step])
        if not OPT["cf"]:
            weights_second(0)
        second_gather(1)
        second_gather(3)
        first_gather(2)
        if OPT["z0"] == 0:
            first_gather(0)
        keyval = jnp.stack(kv[:1] + [land(f"k{step}") for step in range(1, QUAD)])
        start("h1", lambda v: prefix_hop(v, 1), keyval)
        third_gather(1)
        weights_first(1)
        weights(0)
        z1, z3 = all_of(1), None
        up = partial("p01", 0, z1)
        start("a1", lambda v: rotate(v, 1), up)
        third_gather(3)
        second_gather(2)
        z3 = all_of(3)
        down = partial("p03", 0, z3)
        start("a3", lambda v: rotate(v, 3), down)
        weights_second(1)
        near = land("h1")
        start("h2", lambda v: prefix_hop(v, 0), near)
        if OPT["z0"] == 1:
            first_gather(0)
        third_gather(2)
        for step in range(1, QUAD):
            start(f"q{step}", lambda v, step=step: swap(v, step), queries_for(step))
        z2 = all_of(2)
        far = partial("p02", 0, z2)
        start("a2", lambda v: rotate(v, 2), far)
        weights(1)
        up = partial("p11", 1, z1)
        down = partial("p13", 1, z3)
        if OPT["merged"]:
            start("e", lambda v: hop(v, [(0, 1), (3, 2)]), jnp.where(layer == 0, down, up))
            start("b1", lambda v: hop(v, [(0, 1), (1, 2), (2, 3)]), up)
            start("b3", lambda v: hop(v, [(1, 0), (2, 1), (3, 2)]), down)
        else:
            start("b1", lambda v: rotate(v, 1), up)
            start("b3", lambda v: rotate(v, 3), down)
        second_gather(0)
        third_gather(0)
        arrived[0][1], arrived[0][3] = land("a1"), land("a3")
        more = land("e") if OPT["merged"] else None
        far = partial("p12", 1, z2, more=more)
        start("b2", lambda v: rotate(v, 2), far)
        z0 = all_of(0)
        arrived[0][2], arrived[1][1], arrived[1][3] = land("a2"), land("b1"), land("b3")
        arrived[0][0] = partial("p00", 0, z0, dtype=jnp.float32)
        arrived[1][0] = partial("p10", 1, z0, dtype=jnp.float32)
        queries = [queries_for(0)] + [land(f"q{step}") for step in range(1, QUAD)]
        prefix = land("h2")
        prob = weigh(tied("S:s", scalars), queries, keyval, prefix)
        done["S"] = prob
        arrived[1][2] = land("b2")
    else:
        every = lax.all_to_all(grad_y, "head", 0, 1, tiled=True)
        for part in range(len(counts)):
            first = swap(jnp.stack([rows_for(part, mine ^ 1), rows_for(part, mine ^ 3)]), 1)
            second = swap(jnp.stack([rows_for(part, mine ^ 2), first[1]]), 2)
            others[part] = [(first, lambda q: 0), (second, lambda q: 0), (second, lambda q: 1)]
        kv = [keyval_for(step) for step in range(QUAD)]
        keyval = jnp.stack([swap(kv[step], step) if step else kv[0] for step in range(QUAD)])
        prefix = keyval
        for level in reversed(range(levels)):
            prefix = prefix_hop(prefix, level)
        queries = [
            swap(queries_for(step), step) if step else queries_for(step) for step in range(QUAD)
        ]
        for steps in range(layers):
            x = columns(every, (layer - steps) % layers, depth)
            x = rotate(x, -steps) if steps else x
            x = join(x, swap(x, 2))
            for bit in range(head_bits):
                x = join(x, flip(x, 1 << bit))
            x = join(x, swap(x, 1))
            for part in range(len(counts)):
                if steps:
                    arrived[part][steps] = rotate(partial("", part, x), steps)
                else:
                    arrived[part][0] = partial("", part, x, dtype=jnp.float32)
        prob = weigh(scalars, queries, keyval, prefix)

    sums, homes = (), []
    for part, (base, count) in enumerate(zip(bases, counts)):
        terms = [
            arrived[part][steps].reshape(QUAD * sides, share, count * DH) for steps in range(layers)
        ]
        grad_query, *sums = attend(
            tied(f"att{part}:s", scalars), prob, queries, keyval, prefix, terms, base, count, head_bits, tuple(sums)
        )
        done[f"att{part}"] = sums[0]
        homes.append([swap(grad_query[step], step) if step else grad_query[0] for step in range(QUAD)])
    grad_key, grad_value = sums
    if OPT["home"]:
        homes[0] = after(homes[0], grad_key)
    out_query = jnp.zeros(query.shape, query.dtype)
    for base, pieces in zip(bases, homes):
        for step, piece in enumerate(pieces):
            spot = ((mine ^ step) * heads + base) * DH
            out_query = lax.dynamic_update_slice_in_dim(out_query, piece, spot, 1)

    own = QUAD * BLOCK
    both = jnp.concatenate([grad_key, grad_value], axis=1)
    far = both[own:]
    reach = 1
    while 2 * reach < layers:
        hops = [(s, s + reach) for s in range(layers) if (layers - 1 - s) % (2 * reach) == reach]
        far = far + hop(far.astype(jnp.bfloat16), hops).astype(jnp.float32)
        reach *= 2
    narrow = far.astype(jnp.bfloat16)
    near = (both[:own] + jnp.where(layer == layers - 1, far, 0.0)).astype(jnp.bfloat16)
    source = (layers - 1 - reach) * QUAD
    landed = []
    for step in range(QUAD):
        spot = (mine ^ step) * BLOCK
        pairs = [(source + i, (layers - 1) * QUAD + (i ^ step)) for i in range(QUAD)]
        last = lax.ppermute(take(narrow, spot, BLOCK), "ctx", pairs)
        piece = take(near, spot, BLOCK)
        piece = swap(piece, step) if step else piece
        landed.append((piece, last))
    landed = [
        piece.astype(jnp.float32) + last.astype(jnp.float32)
        for piece, last in lax.optimization_barrier(landed)
    ]
    if groups < QUAD:
        added = functools.reduce(jnp.add, landed)
        return out_query, *(x.astype(jnp.bfloat16) for x in jnp.split(added, 2, axis=1))
    totals = [jnp.zeros(key_in.shape, jnp.bfloat16), jnp.zeros(value.shape, jnp.bfloat16)]
    for step, piece in enumerate(landed):
        spot = ((mine ^ step) * groups // QUAD) * DH
        halves = jnp.split(piece.astype(jnp.bfloat16), 2, axis=1)
        totals = [
            lax.dynamic_update_slice_in_dim(total, half, spot, 1)
            for total, half in zip(totals, halves)
        ]
    return out_query, *totals


def solution(mesh):
    placed = (
        P("ctx", "head"),
        P("ctx", "head"),
        P("ctx", "head"),
        P("ctx", "head"),
        P("head", "ctx"),
        P(),
    )
    return jax.shard_map(
        per_device,
        mesh=mesh,
        in_specs=placed,
        out_specs=(P("ctx", "head"), P("ctx", "head"), P("ctx", "head")),
        check_vma=False,
    )
```

```python
import functools

import jax
import jax.numpy as jnp
from jax import lax
from jax.experimental import pallas as pl
from jax.experimental.pallas import tpu as pltpu
from jax.sharding import PartitionSpec as P

OPT = {'vmem': 16, 'cp': 1.0, 'cs': 1.0, 'ca': 1.0, 'cf': 1, 'dual': [0, 0, 0, 1], 'z0': 0, 'merged': 1, 'home': 1, 'cut': 4, 'ties': {'y1:s': ['r3', 'W0a', 'xe2'], 'x3:s': ['r1', 'W0a', 'xe2'], 'r2:s': ['r1', 'r3'], 'k1:s': ['r1', 'y1'], 'k2:s': ['r1'], 'k3:s': ['r1'], 'W1b:s': ['r1'], 'x1:s': ['x3'], 'y3:s': ['y1'], 'c1:s': ['y3', 'r2', 'k1', 'k2', 'k3'], 'c3:s': ['x1', 'r2'], 'y2:s': ['x1', 'y3'], 'y0:s': ['x1', 'y3', 'r2', 'W1b'], 'h1:s': ['x1', 'y3'], 'p01:s': ['h1'], 'p03:s': ['c1'], 'x2:s': ['p01', 'p03'], 'W1a:s': ['y2'], 'c2:s': ['a1', 'y0', 'h1'], 'a3:s': ['x2', 'a1', 'y0', 'h1'], 'x0:s': ['x2', 'a1'], 'h2:s': ['x2', 'a1'], 'p11:s': ['a3', 'W1a', 'x0', 'p02'], 'p13:s': ['p11'], 'c0:s': ['a3'], 'q1:s': ['p02'], 'q2:s': ['p02'], 'q3:s': ['p02'], 'p12:s': ['a2', 'c0', 'h2', 'q1', 'q2', 'q3'], 'p00:s': ['p12'], 'p10:s': ['p12'], 'S:s': ['p12'], 'y1:r': ['r2'], 'att1:s': ['p00']}}
DH = 128
BLOCK = 128
QUAD = 4
SCALE = DH ** (-0.5)
LOG2E = 1.4426950408889634
NT = (((1,), (1,)), ((), ()))


def after(value, *earlier):
    return lax.optimization_barrier((value,) + earlier)[0]


def project_kernel(place_ref, x_ref, *refs):
    w_refs, out_ref = refs[:QUAD], refs[-1]
    mine = place_ref[0]
    width = w_refs[0].shape[1]
    total = refs[QUAD][...].astype(jnp.float32) if len(refs) > QUAD + 1 else None
    for step, w_ref in enumerate(w_refs):
        columns = pl.ds(pl.multiple_of((mine ^ step) * width, width), width)
        term = lax.dot_general(x_ref[:, columns], w_ref[...], NT, preferred_element_type=jnp.float32)
        total = term if total is None else total + term
    out_ref[...] = total.astype(out_ref.dtype)


def project(place, x, w_out, others, base, dtype, more=None):
    rows, depth = x.shape
    _, columns, width = others[0][0].shape
    tile = min(256, columns & -columns)
    steps = columns // tile
    per_place = w_out.shape[0] // QUAD // tile
    offset = base // tile
    out_spec = pl.BlockSpec((rows, tile), lambda n, s: (0, n))
    in_specs = [pl.BlockSpec((rows, depth), lambda n, s: (0, 0))]
    in_specs.append(pl.BlockSpec((tile, width), lambda n, s: (s[0] * per_place + offset + n, 0)))
    for _, pick in others:
        in_specs.append(pl.BlockSpec((None, tile, width), lambda n, s, pick=pick: (pick(s[0]), n, 0)))
    operands = [x, w_out, *(array for array, _ in others)]
    if more is not None:
        in_specs.append(out_spec)
        operands.append(more)
    return pl.pallas_call(
        project_kernel,
        grid_spec=pltpu.PrefetchScalarGridSpec(
            num_scalar_prefetch=1, grid=(steps,), in_specs=in_specs, out_specs=out_spec
        ),
        out_shape=jax.ShapeDtypeStruct((rows, columns), dtype),
        compiler_params=pltpu.CompilerParams(vmem_limit_bytes=OPT['vmem'] * 2**20),
        cost_estimate=pl.CostEstimate(
            flops=int(OPT['cp'] * (2 * rows * depth * columns)),
            bytes_accessed=int(OPT['cp'] * (2 * (rows * depth + depth * columns + rows * columns))),
            transcendentals=0,
        ),
    )(place, *operands)


def lay_out(place_ref, own_ref, late_ref, out):
    for b in range(QUAD):
        out[pl.ds(b * BLOCK, BLOCK), :] = own_ref[b ^ place_ref[0]]
        out[pl.ds((QUAD + b) * BLOCK, BLOCK), :] = late_ref[b ^ place_ref[0]]


def lay_by(place_ref, refs, out):
    for step, ref in enumerate(refs):
        out[pl.ds(pl.multiple_of((step ^ place_ref[0]) * BLOCK, BLOCK), BLOCK), :] = ref[...]


def weigh_kernel(place_ref, k_ref, kp_ref, *refs):
    q_refs, (prob_ref, keys, queries, triangle) = refs[:QUAD], refs[QUAD:]
    mine, root = place_ref[0], place_ref[2]
    own = QUAD * BLOCK
    half = own // 2

    @pl.when(pl.program_id(0) == 0)
    def first():
        lay_out(place_ref, k_ref, kp_ref, keys)
        row = lax.broadcasted_iota(jnp.int32, (half, half), 0)
        col = lax.broadcasted_iota(jnp.int32, (half, half), 1)
        seen = (row // BLOCK > col // BLOCK) | ((row // BLOCK == col // BLOCK) & (row <= col))
        triangle[...] = jnp.where(seen, 0.0, -1e30)

    lay_by(place_ref, q_refs, queries)
    for pair in range(2):
        start = pair * half
        count = 2 * own - start
        q = queries[pl.ds(start, half), :]
        scores = lax.dot_general(
            keys[pl.ds(start, count), :], q, NT, preferred_element_type=jnp.float32
        )
        late = lax.broadcasted_iota(jnp.int32, (own, half), 0) >= root * BLOCK
        parts = [scores[:half] + triangle[...]]
        if pair == 0:
            parts.append(scores[half : 2 * half])
        parts.append(jnp.where(late, scores[count - own :], -1e30))
        scores = jnp.concatenate(parts, axis=0)
        top = jnp.max(scores, axis=0, keepdims=True)
        weights = jnp.exp2((scores - top) * (SCALE * LOG2E))
        prob = weights * (1.0 / jnp.sum(weights, axis=0, keepdims=True))
        prob_ref[0, pl.ds(start, count), pl.ds(start, half)] = prob.astype(jnp.bfloat16)


def weigh(place, queries, keyval, prefix):
    own = QUAD * BLOCK
    block = (QUAD, BLOCK, DH)
    heads = queries[0].shape[1] // DH
    return pl.pallas_call(
        weigh_kernel,
        grid_spec=pltpu.PrefetchScalarGridSpec(
            num_scalar_prefetch=1,
            grid=(heads,),
            in_specs=[
                pl.BlockSpec(block, lambda n, s: (0, 0, 0)),
                pl.BlockSpec(block, lambda n, s: (0, 0, 0)),
            ]
            + [pl.BlockSpec((BLOCK, DH), lambda n, s: (0, n))] * QUAD,
            out_specs=pl.BlockSpec((1, 2 * own, own), lambda n, s: (n, 0, 0)),
            scratch_shapes=[
                pltpu.VMEM((2 * own, DH), jnp.bfloat16),
                pltpu.VMEM((own, DH), jnp.bfloat16),
                pltpu.VMEM((own // 2, own // 2), jnp.float32),
            ],
        ),
        out_shape=jax.ShapeDtypeStruct((heads, 2 * own, own), jnp.bfloat16),
        compiler_params=pltpu.CompilerParams(vmem_limit_bytes=OPT['vmem'] * 2**20),
        cost_estimate=pl.CostEstimate(
            flops=int(OPT['cs'] * (4 * own * own * DH * heads)),
            bytes_accessed=4 * own * own * heads,
            transcendentals=2 * own * own * heads,
        ),
    )(place, keyval, prefix, *queries)


def attend_kernel(head_bits, count_parts, place_ref, prob_ref, k_ref, v_ref, kp_ref, vp_ref, *refs):
    q_refs, refs = refs[:QUAD], refs[QUAD:]
    part_refs, rest = refs[:count_parts], refs[count_parts:]
    gq_ref, dk_ref, dv_ref = rest[-8:-5]
    values, keys_t, keys, queries, grads = rest[-5:]
    before = rest[:-8]
    mine, head_place = place_ref[0], place_ref[1]
    own = QUAD * BLOCK
    half = own // 2
    pieces = 1 << head_bits
    piece = BLOCK // pieces

    @pl.when(pl.program_id(0) == 0)
    def first():
        lay_out(place_ref, k_ref, kp_ref, keys)
        lay_out(place_ref, v_ref, vp_ref, values)
        keys_t[...] = keys[...].astype(jnp.float32).T.astype(jnp.bfloat16)
        if before:
            dk_ref[...] = before[0][...]
            dv_ref[...] = before[1][...]
        else:
            dk_ref[...] = jnp.zeros_like(dk_ref)
            dv_ref[...] = jnp.zeros_like(dv_ref)

    lay_by(place_ref, q_refs, queries)
    for b in range(QUAD):
        for i in range(pieces):
            at = (
                ((b >> 1) ^ (mine >> 1))
                | ((i ^ head_place) << 1)
                | (((b & 1) ^ (mine & 1)) << (1 + head_bits))
            )
            total = part_refs[0][at].astype(jnp.float32)
            for ref in part_refs[1:]:
                total = total + ref[at].astype(jnp.float32)
            grads[pl.ds(b * BLOCK + i * piece, piece), :] = total.astype(jnp.bfloat16)

    for pair in range(2):
        start = pair * half
        q = queries[pl.ds(start, half), :]
        g = grads[pl.ds(start, half), :]
        chunks = [pl.ds(row, half) for row in reversed(range(start, 2 * own, half))]
        lows = [prob_ref[0, rows, pl.ds(start, half)] for rows in chunks]
        dprobs = [
            lax.dot_general(values[rows, :], g, NT, preferred_element_type=jnp.float32)
            for rows in chunks
        ]
        delta = sum(
            jnp.sum(low.astype(jnp.float32) * dprob, axis=0, keepdims=True)
            for low, dprob in zip(lows, dprobs)
        )
        gq = None
        for rows, low, dprob in zip(chunks, lows, dprobs):
            dscore = (low.astype(jnp.float32) * (dprob - delta)).astype(jnp.bfloat16)
            dv_ref[rows, :] += jnp.dot(low, g, preferred_element_type=jnp.float32)
            dk_ref[rows, :] += jnp.dot(dscore, q, preferred_element_type=jnp.float32) * SCALE
            term = jnp.dot(keys_t[:, rows], dscore, preferred_element_type=jnp.float32)
            gq = term if gq is None else gq + term
        gq = (gq * SCALE).T.astype(jnp.bfloat16)
        for b in range(QUAD // 2):
            gq_ref[(pair * (QUAD // 2) + b) ^ mine] = gq[b * BLOCK : (b + 1) * BLOCK]


def attend(place, prob, queries, keyval, prefix, partials, base, heads, head_bits, before=()):
    own = QUAD * BLOCK
    block = (QUAD, BLOCK, DH)
    slots, piece, _ = partials[0].shape

    def column(at):
        return pl.BlockSpec(block, lambda n, s: (0, 0, at))

    whole = pl.BlockSpec((2 * own, DH), lambda n, s: (0, 0))
    return pl.pallas_call(
        functools.partial(attend_kernel, head_bits, len(partials)),
        grid_spec=pltpu.PrefetchScalarGridSpec(
            num_scalar_prefetch=1,
            grid=(heads,),
            in_specs=[
                pl.BlockSpec((1, 2 * own, own), lambda n, s: (base + n, 0, 0)),
                column(0),
                column(1),
                column(0),
                column(1),
            ]
            + [pl.BlockSpec((BLOCK, DH), lambda n, s: (0, base + n))] * QUAD
            + [pl.BlockSpec((slots, piece, DH), lambda n, s: (0, 0, n))] * len(partials)
            + [whole] * len(before),
            out_specs=[pl.BlockSpec(block, lambda n, s: (0, 0, n)), whole, whole],
            scratch_shapes=[
                pltpu.VMEM((2 * own, DH), jnp.bfloat16),
                pltpu.VMEM((DH, 2 * own), jnp.bfloat16),
                pltpu.VMEM((2 * own, DH), jnp.bfloat16),
                pltpu.VMEM((own, DH), jnp.bfloat16),
                pltpu.VMEM((own, DH), jnp.bfloat16),
            ],
        ),
        out_shape=[
            jax.ShapeDtypeStruct((QUAD, BLOCK, heads * DH), jnp.bfloat16),
            jax.ShapeDtypeStruct((2 * own, DH), jnp.float32),
            jax.ShapeDtypeStruct((2 * own, DH), jnp.float32),
        ],
        compiler_params=pltpu.CompilerParams(vmem_limit_bytes=OPT['vmem'] * 2**20),
        cost_estimate=pl.CostEstimate(
            flops=int(OPT['ca'] * (16 * own * own * DH * heads)),
            bytes_accessed=4 * own * own * heads,
            transcendentals=0,
        ),
    )(place, prob, keyval, keyval, prefix, prefix, *queries, *partials, *before)


def per_device(query, key_in, value, grad_y, w_out, parent):
    places, sides = lax.axis_size("ctx"), lax.axis_size("head")
    layers = places // QUAD
    levels = layers.bit_length() - 1
    head_bits = sides.bit_length() - 1
    place, side = lax.axis_index("ctx"), lax.axis_index("head")
    layer, mine = place // QUAD, place % QUAD
    tokens = query.shape[0]
    groups = key_in.shape[1] // DH
    heads = query.shape[1] // DH // QUAD
    depth = QUAD * w_out.shape[1]
    rows = w_out.shape[0] // QUAD
    share = tokens // sides
    counts = [max(1, heads * OPT["cut"] // 8)]
    counts.append(heads - counts[0])
    bases = [sum(counts[:part]) for part in range(len(counts))]

    def swap(x, bits):
        return lax.ppermute(x, "ctx", [(c, c ^ bits) for c in range(places)])

    def flip(x, bits):
        return lax.ppermute(x, "head", [(s, s ^ bits) for s in range(sides)])

    def rotate(x, steps):
        shift = steps * QUAD
        return lax.ppermute(x, "ctx", [(c, (c + shift) % places) for c in range(places)])

    def hop(x, pairs):
        return lax.ppermute(
            x, "ctx", [(s * QUAD + i, t * QUAD + i) for s, t in pairs for i in range(QUAD)]
        )

    def columns(x, at, width):
        return lax.dynamic_slice_in_dim(x, at * width, width, 1)

    def take(x, at, count):
        return lax.dynamic_slice_in_dim(x, at, count, 0)

    def rows_for(part, to):
        return take(w_out, to * rows + bases[part] * DH, counts[part] * DH)

    def join(x, landed):
        return jnp.concatenate([x, landed], axis=0)

    def keyval_for(step):
        at = (mine ^ step) * groups // QUAD
        return jnp.concatenate([columns(key_in, at, DH), columns(value, at, DH)], axis=1)

    def queries_for(step):
        return columns(query, mine ^ step, heads * DH)

    def prefix_hop(prefix, level):
        reach = 1 << level
        sources = [s for s in range(layers) if (layers - 1 - s) % (2 * reach) == 0]
        landed = hop(prefix, [(s, s - reach) for s in sources])
        return jnp.where((layers - 1 - layer) % (2 * reach) == reach, landed, prefix)

    scalars = jnp.stack(
        [
            mine,
            side,
            jnp.where(
                layer == layers - 1,
                QUAD,
                parent[layer * QUAD + QUAD - 1] - (parent.shape[0] - QUAD),
            ),
        ]
    ).astype(jnp.int32)

    done = {}

    def tied(name, x):
        names = [n for n in OPT["ties"].get(name, ()) if n in done]
        if not names:
            return x
        return after(x, *(done[n] for n in names))

    def start(name, send, x):
        done[name] = send(tied(name + ":s", x))

    def land(name):
        done[name] = tied(name + ":r", done[name])
        return done[name]

    def partial(name, part, x, dtype=jnp.bfloat16, more=None):
        done[name] = project(
            tied(name + ":s", scalars), x, w_out, others[part], bases[part] * DH, dtype, more
        )
        return done[name]

    def by_2(x):
        return swap(x, 2)

    def by_1(x):
        return swap(x, 1)

    def by_x(x):
        return flip(x, 1)

    others = [None] * len(counts)
    arrived = [{} for _ in counts]
    if sides == 2 and layers == 4:
        odd = (layer + 1) % 2

        def give(at):
            return lax.dynamic_slice(grad_y, ((1 - side) * share, at * depth), (share, depth))

        def features(steps, other):
            at = (layer - steps) % layers
            held = lax.dynamic_slice(grad_y, (side * share, (at % 2) * depth), (share, depth))
            return jnp.where(at // 2 == side, held, other)

        def interleave(x, landed):
            both = [part.reshape(sides, share, depth) for part in (x, landed)]
            return jnp.stack(both, axis=1).reshape(2 * sides * share, depth)

        def weights_first(part):
            if OPT["cf"]:
                start(f"W{part}b", by_1, jnp.stack([rows_for(part, mine ^ 1), rows_for(part, mine ^ 3)]))
            else:
                first = (mine & 2) ^ 2
                start(f"W{part}a", by_2, jnp.stack([rows_for(part, first + c) for c in range(2)]))

        def weights_second(part):
            if OPT["cf"]:
                beside = land(f"W{part}b")
                start(f"W{part}a", by_2, jnp.stack([rows_for(part, mine ^ 2), beside[1]]))
            else:
                across = land(f"W{part}a")
                through = lax.dynamic_index_in_dim(across, (mine & 1) ^ 1, 0, keepdims=False)
                start(f"W{part}b", by_1, jnp.stack([rows_for(part, mine ^ 1), through]))

        def weights(part):
            if OPT["cf"]:
                across = land(f"W{part}a")
                beside = done[f"W{part}b"]
                others[part] = [(beside, lambda q: 0), (across, lambda q: 0), (across, lambda q: 1)]
            else:
                beside = land(f"W{part}b")
                across = done[f"W{part}a"]
                others[part] = [(beside, lambda q: 0), (across, lambda q: q & 1), (beside, lambda q: 1)]

        x, y, z = {}, {}, {}
        start("xe1", by_x, give(odd))
        weights_first(0)
        start("xe2", by_x, give(1 - odd))
        other = land("xe1")
        start("r1", lambda v: rotate(v, -1), features(1, other))
        start("r3", lambda v: rotate(v, -3), features(3, other))
        if OPT["cf"]:
            weights_second(0)
        other = land("xe2")
        start("r2", lambda v: rotate(v, -2), features(2, other))
        z[0] = features(0, other)

        def first_gather(steps):
            if steps:
                z[steps] = land(f"r{steps}")
            if OPT["dual"][steps]:
                start(f"x{steps}", by_x, z[steps])
            else:
                start(f"y{steps}", by_2, z[steps])

        def second_gather(steps):
            if OPT["dual"][steps]:
                x[steps] = join(z[steps], land(f"x{steps}"))
                start(f"y{steps}", by_2, x[steps])
            else:
                y[steps] = join(z[steps], land(f"y{steps}"))
                start(f"x{steps}", by_x, y[steps])

        def third_gather(steps):
            if OPT["dual"][steps]:
                z[steps] = interleave(x[steps], land(f"y{steps}"))
            else:
                z[steps] = join(y[steps], land(f"x{steps}"))
            start(f"c{steps}", by_1, z[steps])

        def all_of(steps):
            z[steps] = join(z[steps], land(f"c{steps}"))
            return z[steps]

        first_gather(1)
        first_gather(3)
        kv = [keyval_for(step) for step in range(QUAD)]
        for step in range(1, QUAD):
            start(f"k{step}", lambda v, step=step: swap(v, step), kv[step])
        if not OPT["cf"]:
            weights_second(0)
        second_gather(1)
        second_gather(3)
        first_gather(2)
        if OPT["z0"] == 0:
            first_gather(0)
        keyval = jnp.stack(kv[:1] + [land(f"k{step}") for step in range(1, QUAD)])
        start("h1", lambda v: prefix_hop(v, 1), keyval)
        third_gather(1)
        weights_first(1)
        weights(0)
        z1, z3 = all_of(1), None
        up = partial("p01", 0, z1)
        start("a1", lambda v: rotate(v, 1), up)
        third_gather(3)
        second_gather(2)
        z3 = all_of(3)
        down = partial("p03", 0, z3)
        start("a3", lambda v: rotate(v, 3), down)
        weights_second(1)
        near = land("h1")
        start("h2", lambda v: prefix_hop(v, 0), near)
        if OPT["z0"] == 1:
            first_gather(0)
        third_gather(2)
        for step in range(1, QUAD):
            start(f"q{step}", lambda v, step=step: swap(v, step), queries_for(step))
        z2 = all_of(2)
        far = partial("p02", 0, z2)
        start("a2", lambda v: rotate(v, 2), far)
        weights(1)
        up = partial("p11", 1, z1)
        down = partial("p13", 1, z3)
        if OPT["merged"]:
            start("e", lambda v: hop(v, [(0, 1), (3, 2)]), jnp.where(layer == 0, down, up))
            start("b1", lambda v: hop(v, [(0, 1), (1, 2), (2, 3)]), up)
            start("b3", lambda v: hop(v, [(1, 0), (2, 1), (3, 2)]), down)
        else:
            start("b1", lambda v: rotate(v, 1), up)
            start("b3", lambda v: rotate(v, 3), down)
        second_gather(0)
        third_gather(0)
        arrived[0][1], arrived[0][3] = land("a1"), land("a3")
        more = land("e") if OPT["merged"] else None
        far = partial("p12", 1, z2, more=more)
        start("b2", lambda v: rotate(v, 2), far)
        z0 = all_of(0)
        arrived[0][2], arrived[1][1], arrived[1][3] = land("a2"), land("b1"), land("b3")
        arrived[0][0] = partial("p00", 0, z0, dtype=jnp.float32)
        arrived[1][0] = partial("p10", 1, z0, dtype=jnp.float32)
        queries = [queries_for(0)] + [land(f"q{step}") for step in range(1, QUAD)]
        prefix = land("h2")
        prob = weigh(tied("S:s", scalars), queries, keyval, prefix)
        done["S"] = prob
        arrived[1][2] = land("b2")
    else:
        every = lax.all_to_all(grad_y, "head", 0, 1, tiled=True)
        for part in range(len(counts)):
            first = swap(jnp.stack([rows_for(part, mine ^ 1), rows_for(part, mine ^ 3)]), 1)
            second = swap(jnp.stack([rows_for(part, mine ^ 2), first[1]]), 2)
            others[part] = [(first, lambda q: 0), (second, lambda q: 0), (second, lambda q: 1)]
        kv = [keyval_for(step) for step in range(QUAD)]
        keyval = jnp.stack([swap(kv[step], step) if step else kv[0] for step in range(QUAD)])
        prefix = keyval
        for level in reversed(range(levels)):
            prefix = prefix_hop(prefix, level)
        queries = [
            swap(queries_for(step), step) if step else queries_for(step) for step in range(QUAD)
        ]
        for steps in range(layers):
            x = columns(every, (layer - steps) % layers, depth)
            x = rotate(x, -steps) if steps else x
            x = join(x, swap(x, 2))
            for bit in range(head_bits):
                x = join(x, flip(x, 1 << bit))
            x = join(x, swap(x, 1))
            for part in range(len(counts)):
                if steps:
                    arrived[part][steps] = rotate(partial("", part, x), steps)
                else:
                    arrived[part][0] = partial("", part, x, dtype=jnp.float32)
        prob = weigh(scalars, queries, keyval, prefix)

    sums, homes = (), []
    for part, (base, count) in enumerate(zip(bases, counts)):
        terms = [
            arrived[part][steps].reshape(QUAD * sides, share, count * DH) for steps in range(layers)
        ]
        grad_query, *sums = attend(
            tied(f"att{part}:s", scalars), prob, queries, keyval, prefix, terms, base, count, head_bits, tuple(sums)
        )
        done[f"att{part}"] = sums[0]
        homes.append([swap(grad_query[step], step) if step else grad_query[0] for step in range(QUAD)])
    grad_key, grad_value = sums
    if OPT["home"]:
        homes[0] = after(homes[0], grad_key)
    out_query = jnp.zeros(query.shape, query.dtype)
    for base, pieces in zip(bases, homes):
        for step, piece in enumerate(pieces):
            spot = ((mine ^ step) * heads + base) * DH
            out_query = lax.dynamic_update_slice_in_dim(out_query, piece, spot, 1)

    own = QUAD * BLOCK
    both = jnp.concatenate([grad_key, grad_value], axis=1)
    far = both[own:]
    reach = 1
    while 2 * reach < layers:
        hops = [(s, s + reach) for s in range(layers) if (layers - 1 - s) % (2 * reach) == reach]
        far = far + hop(far.astype(jnp.bfloat16), hops).astype(jnp.float32)
        reach *= 2
    narrow = far.astype(jnp.bfloat16)
    near = (both[:own] + jnp.where(layer == layers - 1, far, 0.0)).astype(jnp.bfloat16)
    source = (layers - 1 - reach) * QUAD
    landed = []
    for step in range(QUAD):
        spot = (mine ^ step) * BLOCK
        pairs = [(source + i, (layers - 1) * QUAD + (i ^ step)) for i in range(QUAD)]
        last = lax.ppermute(take(narrow, spot, BLOCK), "ctx", pairs)
        piece = take(near, spot, BLOCK)
        piece = swap(piece, step) if step else piece
        landed.append((piece, last))
    landed = [
        piece.astype(jnp.float32) + last.astype(jnp.float32)
        for piece, last in lax.optimization_barrier(landed)
    ]
    if groups < QUAD:
        added = functools.reduce(jnp.add, landed)
        return out_query, *(x.astype(jnp.bfloat16) for x in jnp.split(added, 2, axis=1))
    totals = [jnp.zeros(key_in.shape, jnp.bfloat16), jnp.zeros(value.shape, jnp.bfloat16)]
    for step, piece in enumerate(landed):
        spot = ((mine ^ step) * groups // QUAD) * DH
        halves = jnp.split(piece.astype(jnp.bfloat16), 2, axis=1)
        totals = [
            lax.dynamic_update_slice_in_dim(total, half, spot, 1)
            for total, half in zip(totals, halves)
        ]
    return out_query, *totals


def solution(mesh):
    placed = (
        P("ctx", "head"),
        P("ctx", "head"),
        P("ctx", "head"),
        P("ctx", "head"),
        P("head", "ctx"),
        P(),
    )
    return jax.shard_map(
        per_device,
        mesh=mesh,
        in_specs=placed,
        out_specs=(P("ctx", "head"), P("ctx", "head"), P("ctx", "head")),
        check_vma=False,
    )
```

```python
import functools

import jax
import jax.numpy as jnp
from jax import lax
from jax.experimental import pallas as pl
from jax.experimental.pallas import tpu as pltpu
from jax.sharding import PartitionSpec as P

OPT = {'vmem': 16, 'cp': 1.0, 'cs': 1.0, 'ca': 1.0, 'cf': 1, 'dual': [0, 0, 0, 1], 'z0': 0, 'merged': 1, 'home': 1, 'cut': 4, 'ties': {'y1:s': ['r3', 'W0a', 'xe2'], 'x3:s': ['r1', 'W0a', 'xe2'], 'r2:s': ['r1', 'r3'], 'k1:s': ['r1', 'y1'], 'k2:s': ['r1'], 'k3:s': ['r1'], 'W1b:s': ['r1'], 'x1:s': ['x3'], 'y3:s': ['y1'], 'c1:s': ['y3', 'r2', 'k1', 'k2', 'k3'], 'c3:s': ['x1', 'r2'], 'y2:s': ['x1', 'y3'], 'y0:s': ['x1', 'y3', 'r2', 'W1b'], 'h1:s': ['x1', 'y3'], 'p01:s': ['h1'], 'p03:s': ['c1'], 'x2:s': ['p01', 'p03'], 'W1a:s': ['y2'], 'c2:s': ['a1', 'y0', 'h1'], 'a3:s': ['x2', 'a1', 'y0', 'h1'], 'x0:s': ['x2', 'a1'], 'h2:s': ['x2', 'a1'], 'p11:s': ['a3', 'W1a', 'x0', 'p02'], 'p13:s': ['p11'], 'c0:s': ['a3'], 'q1:s': ['p02'], 'q2:s': ['p02'], 'q3:s': ['p02'], 'p12:s': ['a2', 'c0', 'h2', 'q1', 'q2', 'q3'], 'p00:s': ['p12'], 'p10:s': ['p12'], 'S:s': ['p12'], 'y1:r': ['r2'], 'att1:s': ['p00']}}
DH = 128
BLOCK = 128
QUAD = 4
SCALE = DH ** (-0.5)
LOG2E = 1.4426950408889634
NT = (((1,), (1,)), ((), ()))


def after(value, *earlier):
    return lax.optimization_barrier((value,) + earlier)[0]


def project_kernel(place_ref, x_ref, *refs):
    w_refs, out_ref = refs[:QUAD], refs[-1]
    mine = place_ref[0]
    width = w_refs[0].shape[1]
    total = refs[QUAD][...].astype(jnp.float32) if len(refs) > QUAD + 1 else None
    for step, w_ref in enumerate(w_refs):
        columns = pl.ds(pl.multiple_of((mine ^ step) * width, width), width)
        term = lax.dot_general(x_ref[:, columns], w_ref[...], NT, preferred_element_type=jnp.float32)
        total = term if total is None else total + term
    out_ref[...] = total.astype(out_ref.dtype)


def project(place, x, w_out, others, base, dtype, more=None):
    rows, depth = x.shape
    _, columns, width = others[0][0].shape
    tile = min(256, columns & -columns)
    steps = columns // tile
    per_place = w_out.shape[0] // QUAD // tile
    offset = base // tile
    out_spec = pl.BlockSpec((rows, tile), lambda n, s: (0, n))
    in_specs = [pl.BlockSpec((rows, depth), lambda n, s: (0, 0))]
    in_specs.append(pl.BlockSpec((tile, width), lambda n, s: (s[0] * per_place + offset + n, 0)))
    for _, pick in others:
        in_specs.append(pl.BlockSpec((None, tile, width), lambda n, s, pick=pick: (pick(s[0]), n, 0)))
    operands = [x, w_out, *(array for array, _ in others)]
    if more is not None:
        in_specs.append(out_spec)
        operands.append(more)
    return pl.pallas_call(
        project_kernel,
        grid_spec=pltpu.PrefetchScalarGridSpec(
            num_scalar_prefetch=1, grid=(steps,), in_specs=in_specs, out_specs=out_spec
        ),
        out_shape=jax.ShapeDtypeStruct((rows, columns), dtype),
        compiler_params=pltpu.CompilerParams(vmem_limit_bytes=OPT['vmem'] * 2**20),
        cost_estimate=pl.CostEstimate(
            flops=int(OPT['cp'] * (2 * rows * depth * columns)),
            bytes_accessed=int(OPT['cp'] * (2 * (rows * depth + depth * columns + rows * columns))),
            transcendentals=0,
        ),
    )(place, *operands)


def lay_out(place_ref, own_ref, late_ref, out):
    for b in range(QUAD):
        out[pl.ds(b * BLOCK, BLOCK), :] = own_ref[b ^ place_ref[0]]
        out[pl.ds((QUAD + b) * BLOCK, BLOCK), :] = late_ref[b ^ place_ref[0]]


def lay_by(place_ref, refs, out):
    for step, ref in enumerate(refs):
        out[pl.ds(pl.multiple_of((step ^ place_ref[0]) * BLOCK, BLOCK), BLOCK), :] = ref[...]


def weigh_kernel(place_ref, k_ref, kp_ref, *refs):
    q_refs, (prob_ref, keys, queries, triangle) = refs[:QUAD], refs[QUAD:]
    mine, root = place_ref[0], place_ref[2]
    own = QUAD * BLOCK
    half = own // 2

    @pl.when(pl.program_id(0) == 0)
    def first():
        lay_out(place_ref, k_ref, kp_ref, keys)
        row = lax.broadcasted_iota(jnp.int32, (half, half), 0)
        col = lax.broadcasted_iota(jnp.int32, (half, half), 1)
        seen = (row // BLOCK > col // BLOCK) | ((row // BLOCK == col // BLOCK) & (row <= col))
        triangle[...] = jnp.where(seen, 0.0, -1e30)

    lay_by(place_ref, q_refs, queries)
    for pair in range(2):
        start = pair * half
        count = 2 * own - start
        q = queries[pl.ds(start, half), :]
        scores = lax.dot_general(
            keys[pl.ds(start, count), :], q, NT, preferred_element_type=jnp.float32
        )
        late = lax.broadcasted_iota(jnp.int32, (own, half), 0) >= root * BLOCK
        parts = [scores[:half] + triangle[...]]
        if pair == 0:
            parts.append(scores[half : 2 * half])
        parts.append(jnp.where(late, scores[count - own :], -1e30))
        scores = jnp.concatenate(parts, axis=0)
        top = jnp.max(scores, axis=0, keepdims=True)
        weights = jnp.exp2((scores - top) * (SCALE * LOG2E))
        prob = weights * (1.0 / jnp.sum(weights, axis=0, keepdims=True))
        prob_ref[0, pl.ds(start, count), pl.ds(start, half)] = prob.astype(jnp.bfloat16)


def weigh(place, queries, keyval, prefix):
    own = QUAD * BLOCK
    block = (QUAD, BLOCK, DH)
    heads = queries[0].shape[1] // DH
    return pl.pallas_call(
        weigh_kernel,
        grid_spec=pltpu.PrefetchScalarGridSpec(
            num_scalar_prefetch=1,
            grid=(heads,),
            in_specs=[
                pl.BlockSpec(block, lambda n, s: (0, 0, 0)),
                pl.BlockSpec(block, lambda n, s: (0, 0, 0)),
            ]
            + [pl.BlockSpec((BLOCK, DH), lambda n, s: (0, n))] * QUAD,
            out_specs=pl.BlockSpec((1, 2 * own, own), lambda n, s: (n, 0, 0)),
            scratch_shapes=[
                pltpu.VMEM((2 * own, DH), jnp.bfloat16),
                pltpu.VMEM((own, DH), jnp.bfloat16),
                pltpu.VMEM((own // 2, own // 2), jnp.float32),
            ],
        ),
        out_shape=jax.ShapeDtypeStruct((heads, 2 * own, own), jnp.bfloat16),
        compiler_params=pltpu.CompilerParams(vmem_limit_bytes=OPT['vmem'] * 2**20),
        cost_estimate=pl.CostEstimate(
            flops=int(OPT['cs'] * (4 * own * own * DH * heads)),
            bytes_accessed=4 * own * own * heads,
            transcendentals=2 * own * own * heads,
        ),
    )(place, keyval, prefix, *queries)


def attend_kernel(head_bits, count_parts, place_ref, prob_ref, k_ref, v_ref, kp_ref, vp_ref, *refs):
    q_refs, refs = refs[:QUAD], refs[QUAD:]
    part_refs, rest = refs[:count_parts], refs[count_parts:]
    gq_ref, dk_ref, dv_ref = rest[-8:-5]
    values, keys_t, keys, queries, grads = rest[-5:]
    before = rest[:-8]
    mine, head_place = place_ref[0], place_ref[1]
    own = QUAD * BLOCK
    half = own // 2
    pieces = 1 << head_bits
    piece = BLOCK // pieces

    @pl.when(pl.program_id(0) == 0)
    def first():
        lay_out(place_ref, k_ref, kp_ref, keys)
        lay_out(place_ref, v_ref, vp_ref, values)
        keys_t[...] = keys[...].astype(jnp.float32).T.astype(jnp.bfloat16)
        if before:
            dk_ref[...] = before[0][...]
            dv_ref[...] = before[1][...]
        else:
            dk_ref[...] = jnp.zeros_like(dk_ref)
            dv_ref[...] = jnp.zeros_like(dv_ref)

    lay_by(place_ref, q_refs, queries)
    for b in range(QUAD):
        for i in range(pieces):
            at = (
                ((b >> 1) ^ (mine >> 1))
                | ((i ^ head_place) << 1)
                | (((b & 1) ^ (mine & 1)) << (1 + head_bits))
            )
            total = part_refs[0][at].astype(jnp.float32)
            for ref in part_refs[1:]:
                total = total + ref[at].astype(jnp.float32)
            grads[pl.ds(b * BLOCK + i * piece, piece), :] = total.astype(jnp.bfloat16)

    q, g = queries[...], grads[...]
    chunks = [(pl.ds(row, half), own if row else half) for row in reversed(range(0, 2 * own, half))]
    lows = [prob_ref[0, rows, pl.ds(0, width)] for rows, width in chunks]
    dprobs = [
        lax.dot_general(values[rows, :], g[:width], NT, preferred_element_type=jnp.float32)
        for rows, width in chunks
    ]
    sums = [
        jnp.sum(low.astype(jnp.float32) * dprob, axis=0, keepdims=True)
        for low, dprob in zip(lows, dprobs)
    ]
    delta = functools.reduce(jnp.add, sums[:-1])
    delta = jnp.concatenate([delta[:, :half] + sums[-1], delta[:, half:]], axis=1)
    terms = []
    for (rows, width), low, dprob in zip(chunks, lows, dprobs):
        dscore = (low.astype(jnp.float32) * (dprob - delta[:, :width])).astype(jnp.bfloat16)
        dv_ref[rows, :] += jnp.dot(low, g[:width], preferred_element_type=jnp.float32)
        dk_ref[rows, :] += jnp.dot(dscore, q[:width], preferred_element_type=jnp.float32) * SCALE
        terms.append(jnp.dot(keys_t[:, rows], dscore, preferred_element_type=jnp.float32))
    gq = functools.reduce(jnp.add, terms[:-1])
    gq = jnp.concatenate([gq[:, :half] + terms[-1], gq[:, half:]], axis=1)
    gq = (gq * SCALE).T.astype(jnp.bfloat16)
    for b in range(QUAD):
        gq_ref[b ^ mine] = gq[b * BLOCK : (b + 1) * BLOCK]


def attend(place, prob, queries, keyval, prefix, partials, base, heads, head_bits, before=()):
    own = QUAD * BLOCK
    block = (QUAD, BLOCK, DH)
    slots, piece, _ = partials[0].shape

    def column(at):
        return pl.BlockSpec(block, lambda n, s: (0, 0, at))

    whole = pl.BlockSpec((2 * own, DH), lambda n, s: (0, 0))
    return pl.pallas_call(
        functools.partial(attend_kernel, head_bits, len(partials)),
        grid_spec=pltpu.PrefetchScalarGridSpec(
            num_scalar_prefetch=1,
            grid=(heads,),
            in_specs=[
                pl.BlockSpec((1, 2 * own, own), lambda n, s: (base + n, 0, 0)),
                column(0),
                column(1),
                column(0),
                column(1),
            ]
            + [pl.BlockSpec((BLOCK, DH), lambda n, s: (0, base + n))] * QUAD
            + [pl.BlockSpec((slots, piece, DH), lambda n, s: (0, 0, n))] * len(partials)
            + [whole] * len(before),
            out_specs=[pl.BlockSpec(block, lambda n, s: (0, 0, n)), whole, whole],
            scratch_shapes=[
                pltpu.VMEM((2 * own, DH), jnp.bfloat16),
                pltpu.VMEM((DH, 2 * own), jnp.bfloat16),
                pltpu.VMEM((2 * own, DH), jnp.bfloat16),
                pltpu.VMEM((own, DH), jnp.bfloat16),
                pltpu.VMEM((own, DH), jnp.bfloat16),
            ],
        ),
        out_shape=[
            jax.ShapeDtypeStruct((QUAD, BLOCK, heads * DH), jnp.bfloat16),
            jax.ShapeDtypeStruct((2 * own, DH), jnp.float32),
            jax.ShapeDtypeStruct((2 * own, DH), jnp.float32),
        ],
        compiler_params=pltpu.CompilerParams(vmem_limit_bytes=OPT['vmem'] * 2**20),
        cost_estimate=pl.CostEstimate(
            flops=int(OPT['ca'] * (16 * own * own * DH * heads)),
            bytes_accessed=4 * own * own * heads,
            transcendentals=0,
        ),
    )(place, prob, keyval, keyval, prefix, prefix, *queries, *partials, *before)


def per_device(query, key_in, value, grad_y, w_out, parent):
    places, sides = lax.axis_size("ctx"), lax.axis_size("head")
    layers = places // QUAD
    levels = layers.bit_length() - 1
    head_bits = sides.bit_length() - 1
    place, side = lax.axis_index("ctx"), lax.axis_index("head")
    layer, mine = place // QUAD, place % QUAD
    tokens = query.shape[0]
    groups = key_in.shape[1] // DH
    heads = query.shape[1] // DH // QUAD
    depth = QUAD * w_out.shape[1]
    rows = w_out.shape[0] // QUAD
    share = tokens // sides
    counts = [max(1, heads * OPT["cut"] // 8)]
    counts.append(heads - counts[0])
    bases = [sum(counts[:part]) for part in range(len(counts))]

    def swap(x, bits):
        return lax.ppermute(x, "ctx", [(c, c ^ bits) for c in range(places)])

    def flip(x, bits):
        return lax.ppermute(x, "head", [(s, s ^ bits) for s in range(sides)])

    def rotate(x, steps):
        shift = steps * QUAD
        return lax.ppermute(x, "ctx", [(c, (c + shift) % places) for c in range(places)])

    def hop(x, pairs):
        return lax.ppermute(
            x, "ctx", [(s * QUAD + i, t * QUAD + i) for s, t in pairs for i in range(QUAD)]
        )

    def columns(x, at, width):
        return lax.dynamic_slice_in_dim(x, at * width, width, 1)

    def take(x, at, count):
        return lax.dynamic_slice_in_dim(x, at, count, 0)

    def rows_for(part, to):
        return take(w_out, to * rows + bases[part] * DH, counts[part] * DH)

    def join(x, landed):
        return jnp.concatenate([x, landed], axis=0)

    def keyval_for(step):
        at = (mine ^ step) * groups // QUAD
        return jnp.concatenate([columns(key_in, at, DH), columns(value, at, DH)], axis=1)

    def queries_for(step):
        return columns(query, mine ^ step, heads * DH)

    def prefix_hop(prefix, level):
        reach = 1 << level
        sources = [s for s in range(layers) if (layers - 1 - s) % (2 * reach) == 0]
        landed = hop(prefix, [(s, s - reach) for s in sources])
        return jnp.where((layers - 1 - layer) % (2 * reach) == reach, landed, prefix)

    scalars = jnp.stack(
        [
            mine,
            side,
            jnp.where(
                layer == layers - 1,
                QUAD,
                parent[layer * QUAD + QUAD - 1] - (parent.shape[0] - QUAD),
            ),
        ]
    ).astype(jnp.int32)

    done = {}

    def tied(name, x):
        names = [n for n in OPT["ties"].get(name, ()) if n in done]
        if not names:
            return x
        return after(x, *(done[n] for n in names))

    def start(name, send, x):
        done[name] = send(tied(name + ":s", x))

    def land(name):
        done[name] = tied(name + ":r", done[name])
        return done[name]

    def partial(name, part, x, dtype=jnp.bfloat16, more=None):
        done[name] = project(
            tied(name + ":s", scalars), x, w_out, others[part], bases[part] * DH, dtype, more
        )
        return done[name]

    def by_2(x):
        return swap(x, 2)

    def by_1(x):
        return swap(x, 1)

    def by_x(x):
        return flip(x, 1)

    others = [None] * len(counts)
    arrived = [{} for _ in counts]
    if sides == 2 and layers == 4:
        odd = (layer + 1) % 2

        def give(at):
            return lax.dynamic_slice(grad_y, ((1 - side) * share, at * depth), (share, depth))

        def features(steps, other):
            at = (layer - steps) % layers
            held = lax.dynamic_slice(grad_y, (side * share, (at % 2) * depth), (share, depth))
            return jnp.where(at // 2 == side, held, other)

        def interleave(x, landed):
            both = [part.reshape(sides, share, depth) for part in (x, landed)]
            return jnp.stack(both, axis=1).reshape(2 * sides * share, depth)

        def weights_first(part):
            if OPT["cf"]:
                start(f"W{part}b", by_1, jnp.stack([rows_for(part, mine ^ 1), rows_for(part, mine ^ 3)]))
            else:
                first = (mine & 2) ^ 2
                start(f"W{part}a", by_2, jnp.stack([rows_for(part, first + c) for c in range(2)]))

        def weights_second(part):
            if OPT["cf"]:
                beside = land(f"W{part}b")
                start(f"W{part}a", by_2, jnp.stack([rows_for(part, mine ^ 2), beside[1]]))
            else:
                across = land(f"W{part}a")
                through = lax.dynamic_index_in_dim(across, (mine & 1) ^ 1, 0, keepdims=False)
                start(f"W{part}b", by_1, jnp.stack([rows_for(part, mine ^ 1), through]))

        def weights(part):
            if OPT["cf"]:
                across = land(f"W{part}a")
                beside = done[f"W{part}b"]
                others[part] = [(beside, lambda q: 0), (across, lambda q: 0), (across, lambda q: 1)]
            else:
                beside = land(f"W{part}b")
                across = done[f"W{part}a"]
                others[part] = [(beside, lambda q: 0), (across, lambda q: q & 1), (beside, lambda q: 1)]

        x, y, z = {}, {}, {}
        start("xe1", by_x, give(odd))
        weights_first(0)
        start("xe2", by_x, give(1 - odd))
        other = land("xe1")
        start("r1", lambda v: rotate(v, -1), features(1, other))
        start("r3", lambda v: rotate(v, -3), features(3, other))
        if OPT["cf"]:
            weights_second(0)
        other = land("xe2")
        start("r2", lambda v: rotate(v, -2), features(2, other))
        z[0] = features(0, other)

        def first_gather(steps):
            if steps:
                z[steps] = land(f"r{steps}")
            if OPT["dual"][steps]:
                start(f"x{steps}", by_x, z[steps])
            else:
                start(f"y{steps}", by_2, z[steps])

        def second_gather(steps):
            if OPT["dual"][steps]:
                x[steps] = join(z[steps], land(f"x{steps}"))
                start(f"y{steps}", by_2, x[steps])
            else:
                y[steps] = join(z[steps], land(f"y{steps}"))
                start(f"x{steps}", by_x, y[steps])

        def third_gather(steps):
            if OPT["dual"][steps]:
                z[steps] = interleave(x[steps], land(f"y{steps}"))
            else:
                z[steps] = join(y[steps], land(f"x{steps}"))
            start(f"c{steps}", by_1, z[steps])

        def all_of(steps):
            z[steps] = join(z[steps], land(f"c{steps}"))
            return z[steps]

        first_gather(1)
        first_gather(3)
        kv = [keyval_for(step) for step in range(QUAD)]
        for step in range(1, QUAD):
            start(f"k{step}", lambda v, step=step: swap(v, step), kv[step])
        if not OPT["cf"]:
            weights_second(0)
        second_gather(1)
        second_gather(3)
        first_gather(2)
        if OPT["z0"] == 0:
            first_gather(0)
        keyval = jnp.stack(kv[:1] + [land(f"k{step}") for step in range(1, QUAD)])
        start("h1", lambda v: prefix_hop(v, 1), keyval)
        third_gather(1)
        weights_first(1)
        weights(0)
        z1, z3 = all_of(1), None
        up = partial("p01", 0, z1)
        start("a1", lambda v: rotate(v, 1), up)
        third_gather(3)
        second_gather(2)
        z3 = all_of(3)
        down = partial("p03", 0, z3)
        start("a3", lambda v: rotate(v, 3), down)
        weights_second(1)
        near = land("h1")
        start("h2", lambda v: prefix_hop(v, 0), near)
        if OPT["z0"] == 1:
            first_gather(0)
        third_gather(2)
        for step in range(1, QUAD):
            start(f"q{step}", lambda v, step=step: swap(v, step), queries_for(step))
        z2 = all_of(2)
        far = partial("p02", 0, z2)
        start("a2", lambda v: rotate(v, 2), far)
        weights(1)
        up = partial("p11", 1, z1)
        down = partial("p13", 1, z3)
        if OPT["merged"]:
            start("e", lambda v: hop(v, [(0, 1), (3, 2)]), jnp.where(layer == 0, down, up))
            start("b1", lambda v: hop(v, [(0, 1), (1, 2), (2, 3)]), up)
            start("b3", lambda v: hop(v, [(1, 0), (2, 1), (3, 2)]), down)
        else:
            start("b1", lambda v: rotate(v, 1), up)
            start("b3", lambda v: rotate(v, 3), down)
        second_gather(0)
        third_gather(0)
        arrived[0][1], arrived[0][3] = land("a1"), land("a3")
        more = land("e") if OPT["merged"] else None
        far = partial("p12", 1, z2, more=more)
        start("b2", lambda v: rotate(v, 2), far)
        z0 = all_of(0)
        arrived[0][2], arrived[1][1], arrived[1][3] = land("a2"), land("b1"), land("b3")
        arrived[0][0] = partial("p00", 0, z0, dtype=jnp.float32)
        arrived[1][0] = partial("p10", 1, z0, dtype=jnp.float32)
        queries = [queries_for(0)] + [land(f"q{step}") for step in range(1, QUAD)]
        prefix = land("h2")
        prob = weigh(tied("S:s", scalars), queries, keyval, prefix)
        done["S"] = prob
        arrived[1][2] = land("b2")
    else:
        every = lax.all_to_all(grad_y, "head", 0, 1, tiled=True)
        for part in range(len(counts)):
            first = swap(jnp.stack([rows_for(part, mine ^ 1), rows_for(part, mine ^ 3)]), 1)
            second = swap(jnp.stack([rows_for(part, mine ^ 2), first[1]]), 2)
            others[part] = [(first, lambda q: 0), (second, lambda q: 0), (second, lambda q: 1)]
        kv = [keyval_for(step) for step in range(QUAD)]
        keyval = jnp.stack([swap(kv[step], step) if step else kv[0] for step in range(QUAD)])
        prefix = keyval
        for level in reversed(range(levels)):
            prefix = prefix_hop(prefix, level)
        queries = [
            swap(queries_for(step), step) if step else queries_for(step) for step in range(QUAD)
        ]
        for steps in range(layers):
            x = columns(every, (layer - steps) % layers, depth)
            x = rotate(x, -steps) if steps else x
            x = join(x, swap(x, 2))
            for bit in range(head_bits):
                x = join(x, flip(x, 1 << bit))
            x = join(x, swap(x, 1))
            for part in range(len(counts)):
                if steps:
                    arrived[part][steps] = rotate(partial("", part, x), steps)
                else:
                    arrived[part][0] = partial("", part, x, dtype=jnp.float32)
        prob = weigh(scalars, queries, keyval, prefix)

    sums, homes = (), []
    for part, (base, count) in enumerate(zip(bases, counts)):
        terms = [
            arrived[part][steps].reshape(QUAD * sides, share, count * DH) for steps in range(layers)
        ]
        grad_query, *sums = attend(
            tied(f"att{part}:s", scalars), prob, queries, keyval, prefix, terms, base, count, head_bits, tuple(sums)
        )
        done[f"att{part}"] = sums[0]
        homes.append([swap(grad_query[step], step) if step else grad_query[0] for step in range(QUAD)])
    grad_key, grad_value = sums
    if OPT["home"]:
        homes[0] = after(homes[0], grad_key)
    out_query = jnp.zeros(query.shape, query.dtype)
    for base, pieces in zip(bases, homes):
        for step, piece in enumerate(pieces):
            spot = ((mine ^ step) * heads + base) * DH
            out_query = lax.dynamic_update_slice_in_dim(out_query, piece, spot, 1)

    own = QUAD * BLOCK
    both = jnp.concatenate([grad_key, grad_value], axis=1)
    far = both[own:]
    reach = 1
    while 2 * reach < layers:
        hops = [(s, s + reach) for s in range(layers) if (layers - 1 - s) % (2 * reach) == reach]
        far = far + hop(far.astype(jnp.bfloat16), hops).astype(jnp.float32)
        reach *= 2
    narrow = far.astype(jnp.bfloat16)
    near = (both[:own] + jnp.where(layer == layers - 1, far, 0.0)).astype(jnp.bfloat16)
    source = (layers - 1 - reach) * QUAD
    landed = []
    for step in range(QUAD):
        spot = (mine ^ step) * BLOCK
        pairs = [(source + i, (layers - 1) * QUAD + (i ^ step)) for i in range(QUAD)]
        last = lax.ppermute(take(narrow, spot, BLOCK), "ctx", pairs)
        piece = take(near, spot, BLOCK)
        piece = swap(piece, step) if step else piece
        landed.append((piece, last))
    landed = [
        piece.astype(jnp.float32) + last.astype(jnp.float32)
        for piece, last in lax.optimization_barrier(landed)
    ]
    if groups < QUAD:
        added = functools.reduce(jnp.add, landed)
        return out_query, *(x.astype(jnp.bfloat16) for x in jnp.split(added, 2, axis=1))
    totals = [jnp.zeros(key_in.shape, jnp.bfloat16), jnp.zeros(value.shape, jnp.bfloat16)]
    for step, piece in enumerate(landed):
        spot = ((mine ^ step) * groups // QUAD) * DH
        halves = jnp.split(piece.astype(jnp.bfloat16), 2, axis=1)
        totals = [
            lax.dynamic_update_slice_in_dim(total, half, spot, 1)
            for total, half in zip(totals, halves)
        ]
    return out_query, *totals


def solution(mesh):
    placed = (
        P("ctx", "head"),
        P("ctx", "head"),
        P("ctx", "head"),
        P("ctx", "head"),
        P("head", "ctx"),
        P(),
    )
    return jax.shard_map(
        per_device,
        mesh=mesh,
        in_specs=placed,
        out_specs=(P("ctx", "head"), P("ctx", "head"), P("ctx", "head")),
        check_vma=False,
    )
```
